32 devices in a mesh: nodes: 16 (over z, y, x), heads: 2 (over core).
Axes of the slice: x: 2, y: 2, z: 4, core: 2. Of those that a mesh axis runs over, the one named last changes fastest.
Arguments:
- features: bfloat16 [12288, 512], P(('nodes', 'heads')), may hold values from -24 to 24
- w_qkv: bfloat16 [512, 3, 512], replicated, may hold values from -0.25 to 0.25
- w_out: bfloat16 [512, 512], replicated, may hold values from -0.25 to 0.25
- w_up: bfloat16 [512, 1024], replicated, may hold values from -0.25 to 0.25
- w_down: bfloat16 [1024, 512], replicated, may hold values from -0.1875 to 0.1875
- pattern: int32 [96, 128, 8], P(('nodes', 'heads')), may hold values from 0 to 65535
- partner: int32 [96, 4], P(('nodes', 'heads')), may hold values from 0 to 2, as said below
- counts: int32 [32], P(('nodes', 'heads')), may hold values from 1 to 3, as said below
Outputs:
- mixed: bfloat16 [12288, 512], P(('nodes', 'heads'))
The draws below stay inside these ranges and needn't reach their ends.
Inputs may be any that keep to these rules, and one draw needn't show every extreme that they name: `partner`: each link of block slot s of device d names a live block slot of device d XOR 2**b_l; every live slot of that device is named by some slot of d. `counts`: some device holds 3 live blocks.
All inputs are finite; a program needn't handle non-finite values.
Results may differ from the reference program's by a relative error of at most 0.012.
The reference program's roundings to bfloat16 on the way (of `projected`, `weights`, `attended` and `hidden`) count: a program that leaves them out, or rounds other values in their place, can miss the bound.
Values may be sent and summed in bfloat16 or wider, within the bound.
A program may use at most 64 MiB of HBM per device.

```python
import jax
import jax.numpy as jnp
from jax import lax

D = 512
H = 8
FF = 1024
BLK = 128
SLOTS = 3
NBLKS = 96
NODES = 12288
DEVICES = 32


def live_counts(key):
    base = jax.random.randint(jax.random.fold_in(key, 101), (DEVICES,), max(1, SLOTS // 3), SLOTS + 1)
    fullest = jax.random.randint(jax.random.fold_in(key, 102), (), 0, DEVICES)
    return jnp.where(jnp.arange(DEVICES) == fullest, SLOTS, base).astype(jnp.int32)


def draw_counts(key, part):
    return live_counts(key)


def draw_partner(key, part):
    live = live_counts(key)
    key = jax.random.fold_in(key, 7)
    log_size = DEVICES.bit_length() - 1
    device = jnp.arange(DEVICES).astype(jnp.int32)
    columns = []
    for link_index in range(4):
        linked_dev = jnp.bitwise_xor(device, 1 << link_index * log_size // 4)
        row_keys = jax.random.split(jax.random.fold_in(key, link_index), DEVICES)
        orders = jax.vmap(lambda one_key: jax.random.permutation(one_key, SLOTS))(row_keys).astype(jnp.int32)
        columns.append(orders % live[linked_dev][:, None])
    return jnp.stack(columns, axis=-1).reshape(NBLKS, 4).astype(jnp.int32)


def draw_features(key, part):
    key = jax.random.fold_in(key, 11)
    position = jnp.arange(D).astype(jnp.float32) / (D - 1)
    column_factor = 0.6 + 0.8 * jax.random.uniform(jax.random.fold_in(key, 1), (D,), jnp.float32)
    base = jnp.clip(jax.random.normal(jax.random.fold_in(key, 2), (NODES, D), jnp.float32), -4.0, 4.0)
    rise = 3.0 ** position
    return (base * rise * column_factor).astype(jnp.bfloat16)


def touch_ends(array, rng, low, top_value):
    index_at = [jax.random.randint(jax.random.fold_in(rng, axis), (), 0, length) for axis, length in enumerate(array.shape)]
    widest = array.shape.index(max(array.shape))
    beside = index_at[:widest] + [(index_at[widest] + 1) % array.shape[widest]] + index_at[widest + 1:]
    return array.at[tuple(index_at)].set(low).at[tuple(beside)].set(top_value)


def bell_draw(stream_key, dims, scale, bound, kind=jnp.bfloat16):
    array = scale * jax.random.normal(stream_key, dims, jnp.float32)
    return jnp.clip(array, min=-bound, max=bound).astype(kind)


def setup_inputs(seed: int = 0) -> dict:
    key_of = jax.random.split(jax.random.key(seed), 9)
    features = draw_features(jax.random.fold_in(key_of[8], 71), 0)
    w_qkv = bell_draw(key_of[1], (D, 3, D), D ** -0.5, 0.25)
    w_out = bell_draw(key_of[2], (D, D), D ** -0.5, 0.25)
    w_up = bell_draw(key_of[3], (D, FF), D ** -0.5, 0.25)
    w_down = bell_draw(key_of[4], (FF, D), FF ** -0.5, 0.1875)
    pattern = touch_ends(jax.random.randint(key_of[5], (NBLKS, BLK, BLK // 16), 0, 65536), jax.random.fold_in(key_of[5], 1), 0, 65535).astype(jnp.int32)
    partner = draw_partner(jax.random.fold_in(key_of[8], 71), 0)
    counts = draw_counts(jax.random.fold_in(key_of[8], 71), 0)
    return dict(features=features, w_qkv=w_qkv, w_out=w_out, w_up=w_up, w_down=w_down, pattern=pattern, partner=partner, counts=counts)


epsilon = 1e-05

def unpack_bits(pattern_words, width):
    column = jnp.arange(width).astype(jnp.int32)
    picked = pattern_words[..., column // 16]
    bits = jnp.right_shift(picked, column % 16) & 1
    return (bits == 1) | jnp.eye(width, dtype=bool)

def reference(features, w_qkv, w_out, w_up, w_down, pattern, partner, counts):
    head_size = D // H
    projected = jnp.dot(features, w_qkv.reshape(D, 3 * D), preferred_element_type=jnp.float32)
    projected = projected.reshape(NODES, 3, D).astype(jnp.bfloat16)
    blocks = projected.reshape(NBLKS, BLK, 3, D)
    log_size = DEVICES.bit_length() - 1
    block_ids = jnp.arange(NBLKS).astype(jnp.int32)
    device = block_ids // SLOTS
    linked = jnp.stack([jnp.bitwise_xor(device, 1 << link_index * log_size // 4) * SLOTS + partner[:, link_index] for link_index in range(4)], axis=1).astype(jnp.int32)
    allowed_local = unpack_bits(pattern, BLK)
    score_scale = 1.0 / head_size ** 0.5

    def attend(item):
        index, others, local = item
        own = blocks[index]
        far = blocks[others]
        keys_values = jnp.concatenate([own[None, :, 1:], far[:, :, 1:]], axis=0).reshape(5 * BLK, 2, D)
        queries = own[:, 0].reshape(BLK, H, head_size).astype(jnp.float32)
        keys = keys_values[:, 0].reshape(5 * BLK, H, head_size).astype(jnp.float32)
        values = keys_values[:, 1].reshape(5 * BLK, H, head_size).astype(jnp.float32)
        scores = jnp.einsum('qhe,khe->hqk', queries, keys) * score_scale
        allowed = jnp.concatenate([local, jnp.ones((BLK, 4 * BLK), dtype=bool)], axis=1)
        scores = jnp.where(allowed[None], scores, -1e+30)
        top_score = lax.optimization_barrier(jnp.max(scores, axis=-1, keepdims=True))
        expo = jnp.exp(scores - top_score)
        weights = (expo / lax.optimization_barrier(jnp.sum(expo, axis=-1, keepdims=True))).astype(jnp.bfloat16)
        result = jnp.einsum('hqk,khe->qhe', weights.astype(jnp.float32), values)
        return result.astype(jnp.bfloat16).reshape(BLK, D)
    attended = lax.map(attend, (block_ids, linked, allowed_local)).reshape(NODES, D)
    resid = features.astype(jnp.float32) + jnp.dot(attended, w_out, preferred_element_type=jnp.float32)
    row_mean = lax.optimization_barrier(jnp.mean(resid, axis=1, keepdims=True))
    row_var = lax.optimization_barrier(jnp.mean(resid * resid, axis=1, keepdims=True)) - row_mean * row_mean
    normed = (resid - row_mean) * lax.rsqrt(row_var + epsilon)
    hidden = jax.nn.relu(jnp.dot(normed.astype(jnp.bfloat16), w_up, preferred_element_type=jnp.float32)).astype(jnp.bfloat16)
    ffn = jnp.dot(hidden, w_down, preferred_element_type=jnp.float32)
    mixed = normed + ffn
    live = block_ids % SLOTS < counts[device]
    live_rows = jnp.repeat(live, BLK)
    return jnp.where(live_rows[:, None], mixed, 0.0).astype(jnp.bfloat16)
```

```python
import functools

import jax
import jax.numpy as jnp
from jax import lax
from jax.experimental import pallas as pl
from jax.experimental.pallas import tpu as pltpu
from jax.sharding import PartitionSpec as P

D = 512
H = 8
HD = D // H
PAIRS = H // 2
LINKS = 4

epsilon = 1e-05
F32 = jnp.float32
BF16 = jnp.bfloat16


def flip(index, mask):
    return index + mask - 2 * mask * ((index // mask) % 2)


def dot_nn(a, b):
    return jnp.dot(a, b, preferred_element_type=F32)


def dot_nt(a, b):
    return lax.dot_general(a, b, (((1,), (1,)), ((), ())), preferred_element_type=F32)


def kernel(
    bits, slots, blk,
    feat_hbm, w3_hbm, wo_hbm, wu_hbm, wd_hbm, pat_hbm, partner, counts,
    out_ref,
    x, w3, wo, wu, wd, pat, wqt, wvt, near, far,
    qpad, kown, vown, knear, vnear, kfar, vfar,
    ob, mb, lb, of, mf, lf, att,
    load_sem, near_send, near_recv, far_send, far_recv,
):
    node = lax.axis_index("nodes")
    core = lax.axis_index("heads")

    def target(bit):
        if bit == 0:
            return (node, flip(core, 1))
        return (flip(node, 2 ** (bit - 1)), core)

    loads = []
    for i, (src, dst) in enumerate(
        [(w3_hbm, w3), (feat_hbm, x), (pat_hbm, pat), (wo_hbm, wo), (wu_hbm, wu), (wd_hbm, wd)]
    ):
        loads.append(pltpu.make_async_copy(src, dst, load_sem.at[i]))
        loads[-1].start()

    barrier = pltpu.get_barrier_semaphore()
    for bit in bits:
        pl.semaphore_signal(
            barrier, inc=1, device_id=target(bit), device_id_type=pl.DeviceIdType.MESH
        )
    pl.semaphore_wait(barrier, LINKS)

    far_copies = []
    near_copy = pltpu.make_async_remote_copy(
        src_ref=feat_hbm, dst_ref=near, send_sem=near_send, recv_sem=near_recv,
        device_id=target(bits[0]), device_id_type=pl.DeviceIdType.MESH,
    )
    for j in range(slots):
        row = []
        for l in range(LINKS - 1):
            row.append(pltpu.make_async_remote_copy(
                src_ref=feat_hbm.at[pl.ds(j * blk, blk)],
                dst_ref=far.at[j, pl.ds(l * blk, blk)],
                send_sem=far_send.at[j, l], recv_sem=far_recv.at[j, l],
                device_id=target(bits[l + 1]), device_id_type=pl.DeviceIdType.MESH,
            ))
            row[-1].start()
        far_copies.append(row)
        if j == 0:
            near_copy.start()

    loads[0].wait()
    loads[1].wait()
    wqt[...] = w3[0].T
    wvt[...] = w3[2].T
    own = x[...]
    qt = dot_nt(wqt[...], own).astype(BF16) * jnp.asarray(1.0 / HD**0.5, BF16)
    zero = jnp.zeros((HD, blk), BF16)
    for s in range(slots):
        for p in range(PAIRS):
            a = qt[2 * p * HD : (2 * p + 1) * HD, s * blk : (s + 1) * blk]
            b = qt[(2 * p + 1) * HD : (2 * p + 2) * HD, s * blk : (s + 1) * blk]
            qpad[s, p] = jnp.concatenate(
                [jnp.concatenate([a, zero], 1), jnp.concatenate([zero, b], 1)], 0
            )

    def project(rows, put_k, put_v):
        k = dot_nn(rows, w3[1]).astype(BF16)
        v = dot_nt(wvt[...], rows).astype(BF16)
        for i in range(slots):
            put_k(i, k[i * blk : (i + 1) * blk])
            put_v(i, v[:, i * blk : (i + 1) * blk])

    def setter(ref, where):
        def put(i, value):
            ref[where(i)] = value
        return put

    project(own, setter(kown, lambda i: i), setter(vown, lambda i: i))
    near_copy.wait_recv()
    project(near[...], setter(knear, lambda i: i), setter(vnear, lambda i: i))
    loads[2].wait()

    def keep(o, m, l, o_ref, m_ref, l_ref, at, p):
        o_ref[at + (pl.ds(2 * p * HD, HD),)] = o[:HD, :blk]
        o_ref[at + (pl.ds((2 * p + 1) * HD, HD),)] = o[HD:, blk:]
        for half in range(2):
            cols = slice(half * blk, (half + 1) * blk)
            m_ref[at + (pl.ds(2 * p + half, 1),)] = m[:, cols]
            l_ref[at + (pl.ds(2 * p + half, 1),)] = l[:, cols]

    bit_row = lax.broadcasted_iota(jnp.int32, (16, blk), 0)
    key_at = lax.broadcasted_iota(jnp.int32, (blk, blk), 0)
    query_at = lax.broadcasted_iota(jnp.int32, (blk, blk), 1)
    for s in range(slots):
        words = pat[s]
        picked = jnp.concatenate(
            [
                jnp.right_shift(jnp.broadcast_to(words[w : w + 1], (16, blk)), bit_row) & 1
                for w in range(blk // 16)
            ],
            0,
        )
        bias = jnp.where((picked == 1) | (key_at == query_at), 0.0, -1e30).astype(F32)
        bias = jnp.concatenate([bias, bias], 1)
        linked = partner[s, 0]
        k1 = knear[linked]
        v1 = vnear[linked]
        for p in range(PAIRS):
            cols = slice(2 * p * HD, 2 * (p + 1) * HD)
            q = qpad[s, p]
            s0 = dot_nn(kown[s, :, cols], q) + bias
            s1 = dot_nn(k1[:, cols], q)
            m = jnp.maximum(jnp.max(s0, 0, keepdims=True), jnp.max(s1, 0, keepdims=True))
            e0 = jnp.exp(s0 - m)
            e1 = jnp.exp(s1 - m)
            l = jnp.sum(e0, 0, keepdims=True) + jnp.sum(e1, 0, keepdims=True)
            o = dot_nn(
                jnp.concatenate([vown[s, cols], v1[cols]], 1),
                jnp.concatenate([e0.astype(BF16), e1.astype(BF16)], 0),
            )
            keep(o, m, l, ob, mb, lb, (s,), p)

    ranks, order = [], []
    for l in range(1, LINKS):
        named = [partner[s, l] for s in range(slots)]
        rank = []
        for s in range(slots):
            r = jnp.int32(0)
            for t in range(slots):
                if t != s:
                    before = named[t] <= named[s] if t < s else named[t] < named[s]
                    r = r + jnp.where(before, 1, 0).astype(jnp.int32)
            rank.append(r)
        at = []
        for j in range(slots):
            slot, block = jnp.int32(0), jnp.int32(0)
            for s in range(slots):
                slot = jnp.where(rank[s] == j, s, slot)
                block = jnp.where(rank[s] == j, named[s], block)
            at.append((slot, block))
        ranks.append(rank)
        order.append(at)

    for j in range(slots):
        for l in range(LINKS - 1):
            far_copies[j][l].wait_recv()
        rows = far[j]
        k = dot_nn(rows, w3[1]).astype(BF16)
        v = dot_nt(wvt[...], rows).astype(BF16)
        for l in range(LINKS - 1):
            kfar[l, j] = k[l * blk : (l + 1) * blk]
            vfar[l, j] = v[:, l * blk : (l + 1) * blk]
        for l in range(LINKS - 1):
            slot, block = order[l][j]
            kj = kfar[l, block]
            vj = vfar[l, block]
            for p in range(PAIRS):
                cols = slice(2 * p * HD, 2 * (p + 1) * HD)
                scores = dot_nn(kj[:, cols], qpad[slot, p])
                m = jnp.max(scores, 0, keepdims=True)
                e = jnp.exp(scores - m)
                o = dot_nn(vj[cols], e.astype(BF16))
                keep(o, m, jnp.sum(e, 0, keepdims=True), of, mf, lf, (l, j), p)

    for s in range(slots):
        ms = [mb[s]] + [mf[l, ranks[l][s]] for l in range(LINKS - 1)]
        ls = [lb[s]] + [lf[l, ranks[l][s]] for l in range(LINKS - 1)]
        os = [ob[s]] + [of[l, ranks[l][s]] for l in range(LINKS - 1)]
        top = functools.reduce(jnp.maximum, ms)
        scale = [jnp.exp(m - top) for m in ms]
        total = functools.reduce(jnp.add, [a * b for a, b in zip(scale, ls)])
        scale = [a / total for a in scale]
        heads = []
        for h in range(H):
            heads.append(functools.reduce(
                jnp.add,
                [o[h * HD : (h + 1) * HD] * a[h : h + 1] for o, a in zip(os, scale)],
            ))
        joined = jnp.concatenate(heads, 0)
        att[pl.ds(s * blk, blk)] = joined.T.astype(BF16)

    for i in (3, 4, 5):
        loads[i].wait()
    resid = x[...].astype(F32) + dot_nn(att[...], wo[...])
    mean = jnp.mean(resid, 1, keepdims=True)
    var = jnp.mean(resid * resid, 1, keepdims=True) - mean * mean
    normed = (resid - mean) * lax.rsqrt(var + epsilon)
    hidden = jnp.maximum(dot_nn(normed.astype(BF16), wu[...]), 0.0).astype(BF16)
    mixed = normed + dot_nn(hidden, wd[...])
    live = counts[0]
    for s in range(slots):
        part = mixed[s * blk : (s + 1) * blk]
        out_ref[pl.ds(s * blk, blk)] = jnp.where(s < live, part, 0.0).astype(BF16)

    near_copy.wait_send()
    for row in far_copies:
        for copy in row:
            copy.wait_send()


def local(features, w_qkv, w_out, w_up, w_down, pattern, partner, counts):
    rows, width = features.shape
    slots = partner.shape[0]
    blk = rows // slots
    ff = w_up.shape[1]
    words = pattern.shape[2]
    log_size = (lax.axis_size("nodes") * lax.axis_size("heads")).bit_length() - 1
    bits = [i * log_size // 4 for i in range(LINKS)]
    far = LINKS - 1
    any_spec = pl.BlockSpec(memory_space=pl.ANY)
    smem = pl.BlockSpec(memory_space=pltpu.SMEM)
    vm = pltpu.VMEM
    sem = pltpu.SemaphoreType.DMA
    return pl.pallas_call(
        functools.partial(kernel, bits, slots, blk),
        out_shape=jax.ShapeDtypeStruct((rows, width), BF16),
        in_specs=[any_spec] * 6 + [smem] * 2,
        out_specs=pl.BlockSpec(memory_space=pltpu.VMEM),
        scratch_shapes=[
            vm((rows, width), BF16),
            vm((3, width, width), BF16),
            vm((width, width), BF16),
            vm((width, ff), BF16),
            vm((ff, width), BF16),
            vm((slots, words, blk), jnp.int32),
            vm((width, width), BF16),
            vm((width, width), BF16),
            vm((rows, width), BF16),
            vm((slots, far * blk, width), BF16),
            vm((slots, PAIRS, 2 * HD, 2 * blk), BF16),
            vm((slots, blk, width), BF16),
            vm((slots, width, blk), BF16),
            vm((slots, blk, width), BF16),
            vm((slots, width, blk), BF16),
            vm((far, slots, blk, width), BF16),
            vm((far, slots, width, blk), BF16),
            vm((slots, width, blk), F32),
            vm((slots, H, blk), F32),
            vm((slots, H, blk), F32),
            vm((far, slots, width, blk), F32),
            vm((far, slots, H, blk), F32),
            vm((far, slots, H, blk), F32),
            vm((rows, width), BF16),
            sem((6,)),
            sem,
            sem,
            sem((slots, far)),
            sem((slots, far)),
        ],
        compiler_params=pltpu.CompilerParams(
            collective_id=0, has_side_effects=True, vmem_limit_bytes=60 * 2**20
        ),
        cost_estimate=pl.CostEstimate(
            flops=5 * 10**9, bytes_accessed=10 * 2**20, transcendentals=2 * 10**6
        ),
        name="layer",
    )(
        features, jnp.transpose(w_qkv, (1, 0, 2)), w_out, w_up, w_down,
        jnp.transpose(pattern, (0, 2, 1)), partner, counts,
    )


def solution(mesh):
    placed = (
        P(("nodes", "heads"), None),
        P(),
        P(),
        P(),
        P(),
        P(("nodes", "heads"), None, None),
        P(("nodes", "heads"), None),
        P(("nodes", "heads")),
    )
    return jax.shard_map(
        local, mesh=mesh, in_specs=placed, out_specs=P(("nodes", "heads"), None), check_vma=False
    )
```

```python
import functools

import jax
import jax.numpy as jnp
from jax import lax
from jax.experimental import pallas as pl
from jax.experimental.pallas import tpu as pltpu
from jax.sharding import PartitionSpec as P

D = 512
H = 8
HD = D // H
PAIRS = H // 2
LINKS = 4

epsilon = 1e-05
F32 = jnp.float32
BF16 = jnp.bfloat16


def flip(index, mask):
    return index + mask - 2 * mask * ((index // mask) % 2)


def dot_nn(a, b):
    return jnp.dot(a, b, preferred_element_type=F32)


def dot_nt(a, b):
    return lax.dot_general(a, b, (((1,), (1,)), ((), ())), preferred_element_type=F32)


def kernel(
    bits, slots, blk,
    feat_hbm, w3_hbm, wo_hbm, wu_hbm, wd_hbm, pat_hbm, partner_hbm, counts,
    out_ref,
    partner, x, w3, wo, wu, wd, pat, wqt, wvt, near, far,
    qpad, kown, vown, knear, vnear, kfar, vfar,
    ob, mb, lb, of, mf, lf, att,
    load_sem, near_send, near_recv, far_send, far_recv,
):
    node = lax.axis_index("nodes")
    core = lax.axis_index("heads")

    def target(bit):
        if bit == 0:
            return (node, flip(core, 1))
        return (flip(node, 2 ** (bit - 1)), core)

    loads = []
    for i, (src, dst) in enumerate(
        [(w3_hbm, w3), (feat_hbm, x), (pat_hbm, pat), (wo_hbm, wo), (wu_hbm, wu), (wd_hbm, wd),
         (partner_hbm, partner)]
    ):
        loads.append(pltpu.make_async_copy(src, dst, load_sem.at[i]))
        loads[-1].start()

    barrier = pltpu.get_barrier_semaphore()
    for bit in bits:
        pl.semaphore_signal(
            barrier, inc=1, device_id=target(bit), device_id_type=pl.DeviceIdType.MESH
        )
    pl.semaphore_wait(barrier, LINKS)

    far_copies = []
    near_copy = pltpu.make_async_remote_copy(
        src_ref=feat_hbm, dst_ref=near, send_sem=near_send, recv_sem=near_recv,
        device_id=target(bits[0]), device_id_type=pl.DeviceIdType.MESH,
    )
    for j in range(slots):
        row = []
        for l in range(LINKS - 1):
            row.append(pltpu.make_async_remote_copy(
                src_ref=feat_hbm.at[pl.ds(j * blk, blk)],
                dst_ref=far.at[j, pl.ds(l * blk, blk)],
                send_sem=far_send.at[j, l], recv_sem=far_recv.at[j, l],
                device_id=target(bits[l + 1]), device_id_type=pl.DeviceIdType.MESH,
            ))
            row[-1].start()
        far_copies.append(row)
        if j == 0:
            near_copy.start()

    loads[0].wait()
    loads[1].wait()
    wqt[...] = w3[0].T
    wvt[...] = w3[2].T
    own = x[...]
    qt = dot_nt(wqt[...], own).astype(BF16) * jnp.asarray(1.0 / HD**0.5, BF16)
    zero = jnp.zeros((HD, blk), BF16)
    for s in range(slots):
        for p in range(PAIRS):
            a = qt[2 * p * HD : (2 * p + 1) * HD, s * blk : (s + 1) * blk]
            b = qt[(2 * p + 1) * HD : (2 * p + 2) * HD, s * blk : (s + 1) * blk]
            qpad[s, p] = jnp.concatenate(
                [jnp.concatenate([a, zero], 1), jnp.concatenate([zero, b], 1)], 0
            )

    def project(rows, put_k, put_v):
        k = dot_nn(rows, w3[1]).astype(BF16)
        v = dot_nt(wvt[...], rows).astype(BF16)
        for i in range(slots):
            put_k(i, k[i * blk : (i + 1) * blk])
            put_v(i, v[:, i * blk : (i + 1) * blk])

    def setter(ref, where):
        def put(i, value):
            ref[where(i)] = value
        return put

    project(own, setter(kown, lambda i: i), setter(vown, lambda i: i))
    near_copy.wait_recv()
    project(near[...], setter(knear, lambda i: i), setter(vnear, lambda i: i))
    for i in (2, 6):
        loads[i].wait()

    def run(units):
        waiting = None
        scores = units[0][0]()
        for i, (_, values, put) in enumerate(units):
            following = units[i + 1][0]() if i + 1 < len(units) else None
            m = functools.reduce(jnp.maximum, [jnp.max(a, 0, keepdims=True) for a in scores])
            expo = [jnp.exp(a - m) for a in scores]
            l = functools.reduce(jnp.add, [jnp.sum(a, 0, keepdims=True) for a in expo])
            expo = [a.astype(BF16) for a in expo]
            if waiting is not None:
                waiting()
            waiting = functools.partial(
                lambda values, put, expo, m, l: put(values(expo), m, l), values, put, expo, m, l
            )
            scores = following
        waiting()

    def keep(o_ref, m_ref, l_ref, at, p, o, m, l):
        o_ref[at + (pl.ds(2 * p * HD, HD),)] = o[:HD, :blk]
        o_ref[at + (pl.ds((2 * p + 1) * HD, HD),)] = o[HD:, blk:]
        for half in range(2):
            cols = slice(half * blk, (half + 1) * blk)
            m_ref[at + (pl.ds(2 * p + half, 1),)] = m[:, cols]
            l_ref[at + (pl.ds(2 * p + half, 1),)] = l[:, cols]

    bit_row = lax.broadcasted_iota(jnp.int32, (16, blk), 0)
    key_at = lax.broadcasted_iota(jnp.int32, (blk, blk), 0)
    query_at = lax.broadcasted_iota(jnp.int32, (blk, blk), 1)
    units = []
    for s in range(slots):
        words = pat[s]
        picked = jnp.concatenate(
            [
                jnp.right_shift(jnp.broadcast_to(words[w : w + 1], (16, blk)), bit_row) & 1
                for w in range(blk // 16)
            ],
            0,
        )
        bias = jnp.where((picked == 1) | (key_at == query_at), 0.0, -1e30).astype(F32)
        bias = jnp.concatenate([bias, bias], 1)
        linked = partner[s, 0]
        k1 = knear[linked]
        v1 = vnear[linked]
        for p in range(PAIRS):
            cols = slice(2 * p * HD, 2 * (p + 1) * HD)

            def scores(s=s, p=p, cols=cols, bias=bias, k1=k1):
                q = qpad[s, p]
                return [dot_nn(kown[s, :, cols], q) + bias, dot_nn(k1[:, cols], q)]

            def values(e, s=s, cols=cols, v1=v1):
                return dot_nn(
                    jnp.concatenate([vown[s, cols], v1[cols]], 1), jnp.concatenate(e, 0)
                )

            units.append((scores, values, functools.partial(keep, ob, mb, lb, (s,), p)))
    run(units)

    for i in (3, 4, 5):
        loads[i].wait()

    ranks, order = [], []
    for l in range(1, LINKS):
        named = [partner[s, l] for s in range(slots)]
        rank = []
        for s in range(slots):
            r = jnp.int32(0)
            for t in range(slots):
                if t != s:
                    before = named[t] <= named[s] if t < s else named[t] < named[s]
                    r = r + jnp.where(before, 1, 0).astype(jnp.int32)
            rank.append(r)
        at = []
        for j in range(slots):
            slot, block = jnp.int32(0), jnp.int32(0)
            for s in range(slots):
                slot = jnp.where(rank[s] == j, s, slot)
                block = jnp.where(rank[s] == j, named[s], block)
            at.append((slot, block))
        ranks.append(rank)
        order.append(at)

    for j in range(slots):
        for l in range(LINKS - 1):
            far_copies[j][l].wait_recv()
        rows = far[j]
        k = dot_nn(rows, w3[1]).astype(BF16)
        v = dot_nt(wvt[...], rows).astype(BF16)
        for l in range(LINKS - 1):
            kfar[l, j] = k[l * blk : (l + 1) * blk]
            vfar[l, j] = v[:, l * blk : (l + 1) * blk]
        units = []
        for l in range(LINKS - 1):
            slot, block = order[l][j]
            for p in range(PAIRS):
                cols = slice(2 * p * HD, 2 * (p + 1) * HD)

                def scores(l=l, slot=slot, block=block, p=p, cols=cols):
                    return [dot_nn(kfar[l, block, :, cols], qpad[slot, p])]

                def values(e, l=l, block=block, cols=cols):
                    return dot_nn(vfar[l, block, cols], e[0])

                units.append((scores, values, functools.partial(keep, of, mf, lf, (l, j), p)))
        run(units)

    for s in range(slots):
        ms = [mb[s]] + [mf[l, ranks[l][s]] for l in range(LINKS - 1)]
        ls = [lb[s]] + [lf[l, ranks[l][s]] for l in range(LINKS - 1)]
        os = [ob[s]] + [of[l, ranks[l][s]] for l in range(LINKS - 1)]
        top = functools.reduce(jnp.maximum, ms)
        scale = [jnp.exp(m - top) for m in ms]
        total = functools.reduce(jnp.add, [a * b for a, b in zip(scale, ls)])
        scale = [a / total for a in scale]
        heads = []
        for h in range(H):
            heads.append(functools.reduce(
                jnp.add,
                [o[h * HD : (h + 1) * HD] * a[h : h + 1] for o, a in zip(os, scale)],
            ))
        joined = jnp.concatenate(heads, 0)
        att[pl.ds(s * blk, blk)] = joined.astype(BF16).T

    resid = x[...].astype(F32) + dot_nn(att[...], wo[...])
    mean = jnp.mean(resid, 1, keepdims=True)
    var = jnp.mean(resid * resid, 1, keepdims=True) - mean * mean
    normed = (resid - mean) * lax.rsqrt(var + epsilon)
    hidden = jnp.maximum(dot_nn(normed.astype(BF16), wu[...]), 0.0).astype(BF16)
    mixed = normed + dot_nn(hidden, wd[...])
    live = counts[0]
    for s in range(slots):
        part = mixed[s * blk : (s + 1) * blk]
        out_ref[pl.ds(s * blk, blk)] = jnp.where(s < live, part, 0.0).astype(BF16)

    near_copy.wait_send()
    for row in far_copies:
        for copy in row:
            copy.wait_send()


def local(features, w_qkv, w_out, w_up, w_down, pattern, partner, counts):
    rows, width = features.shape
    slots = partner.shape[0]
    blk = rows // slots
    ff = w_up.shape[1]
    words = pattern.shape[2]
    log_size = (lax.axis_size("nodes") * lax.axis_size("heads")).bit_length() - 1
    bits = [i * log_size // 4 for i in range(LINKS)]
    far = LINKS - 1
    any_spec = pl.BlockSpec(memory_space=pl.ANY)
    vm = pltpu.VMEM
    sem = pltpu.SemaphoreType.DMA
    operands = [
        pltpu.with_memory_space_constraint(a, pltpu.HBM)
        for a in (
            features, jnp.transpose(w_qkv, (1, 0, 2)), w_out, w_up, w_down,
            jnp.transpose(pattern, (0, 2, 1)), partner,
        )
    ]
    return pl.pallas_call(
        functools.partial(kernel, bits, slots, blk),
        out_shape=pltpu.VMEM((rows, width), BF16),
        in_specs=[any_spec] * 7 + [pl.BlockSpec(memory_space=pltpu.SMEM)],
        out_specs=pl.BlockSpec(memory_space=pltpu.VMEM),
        scratch_shapes=[
            pltpu.SMEM(partner.shape, jnp.int32),
            vm((rows, width), BF16),
            vm((3, width, width), BF16),
            vm((width, width), BF16),
            vm((width, ff), BF16),
            vm((ff, width), BF16),
            vm((slots, words, blk), jnp.int32),
            vm((width, width), BF16),
            vm((width, width), BF16),
            vm((rows, width), BF16),
            vm((slots, far * blk, width), BF16),
            vm((slots, PAIRS, 2 * HD, 2 * blk), BF16),
            vm((slots, blk, width), BF16),
            vm((slots, width, blk), BF16),
            vm((slots, blk, width), BF16),
            vm((slots, width, blk), BF16),
            vm((far, slots, blk, width), BF16),
            vm((far, slots, width, blk), BF16),
            vm((slots, width, blk), F32),
            vm((slots, H, blk), F32),
            vm((slots, H, blk), F32),
            vm((far, slots, width, blk), F32),
            vm((far, slots, H, blk), F32),
            vm((far, slots, H, blk), F32),
            vm((rows, width), BF16),
            sem((7,)),
            sem,
            sem,
            sem((slots, far)),
            sem((slots, far)),
        ],
        compiler_params=pltpu.CompilerParams(
            collective_id=0, has_side_effects=True, vmem_limit_bytes=48 * 2**20
        ),
        cost_estimate=pl.CostEstimate(
            flops=5 * 10**9, bytes_accessed=10 * 2**20, transcendentals=2 * 10**6
        ),
        name="layer",
    )(*operands, counts)


def solution(mesh):
    placed = (
        P(("nodes", "heads"), None),
        P(),
        P(),
        P(),
        P(),
        P(("nodes", "heads"), None, None),
        P(("nodes", "heads"), None),
        P(("nodes", "heads")),
    )
    return jax.shard_map(
        local, mesh=mesh, in_specs=placed, out_specs=P(("nodes", "heads"), None), check_vma=False
    )
```

```python
import functools

import jax
import jax.numpy as jnp
from jax import lax
from jax.experimental import pallas as pl
from jax.experimental.pallas import tpu as pltpu
from jax.sharding import PartitionSpec as P

D = 512
H = 8
HD = D // H
PAIRS = H // 2
LINKS = 4

epsilon = 1e-05
F32 = jnp.float32
BF16 = jnp.bfloat16


def flip(index, mask):
    return index + mask - 2 * mask * ((index // mask) % 2)


def dot_nn(a, b):
    return jnp.dot(a, b, preferred_element_type=F32)


def dot_nt(a, b):
    return lax.dot_general(a, b, (((1,), (1,)), ((), ())), preferred_element_type=F32)


def kernel(
    bits, slots, blk,
    feat_hbm, w3_hbm, wo_hbm, wu_hbm, wd_hbm, pat_hbm, partner_hbm, counts,
    out_ref,
    partner, x, w3, wo, wu, wd, pat, wqt, wvt, near, far,
    qpad, kown, vown, knear, vnear, kfar, vfar,
    ob, mb, lb, of, mf, lf, nf, nb,
    load_sem, near_send, near_recv, far_send, far_recv,
):
    node = lax.axis_index("nodes")
    core = lax.axis_index("heads")

    def target(bit):
        if bit == 0:
            return (node, flip(core, 1))
        return (flip(node, 2 ** (bit - 1)), core)

    loads = []
    for i, (src, dst) in enumerate(
        [(w3_hbm, w3), (feat_hbm, x), (pat_hbm, pat), (wo_hbm, wo), (wu_hbm, wu), (wd_hbm, wd),
         (partner_hbm, partner)]
    ):
        loads.append(pltpu.make_async_copy(src, dst, load_sem.at[i]))
        loads[-1].start()

    barrier = pltpu.get_barrier_semaphore()
    for bit in bits:
        pl.semaphore_signal(
            barrier, inc=1, device_id=target(bit), device_id_type=pl.DeviceIdType.MESH
        )
    pl.semaphore_wait(barrier, LINKS)

    far_copies = []
    near_copy = pltpu.make_async_remote_copy(
        src_ref=feat_hbm, dst_ref=near, send_sem=near_send, recv_sem=near_recv,
        device_id=target(bits[0]), device_id_type=pl.DeviceIdType.MESH,
    )
    for j in range(slots):
        row = []
        for l in range(LINKS - 1):
            row.append(pltpu.make_async_remote_copy(
                src_ref=feat_hbm.at[pl.ds(j * blk, blk)],
                dst_ref=far.at[j, pl.ds(l * blk, blk)],
                send_sem=far_send.at[j, l], recv_sem=far_recv.at[j, l],
                device_id=target(bits[l + 1]), device_id_type=pl.DeviceIdType.MESH,
            ))
            if j < 2:
                row[-1].start()
        far_copies.append(row)
        if j == 0:
            near_copy.start()

    loads[0].wait()
    loads[1].wait()
    wqt[...] = w3[0].T
    wvt[...] = w3[2].T
    own = x[...]
    qt = dot_nt(wqt[...], own).astype(BF16) * jnp.asarray(1.0 / HD**0.5, BF16)
    zero = jnp.zeros((HD, blk), BF16)
    for s in range(slots):
        for p in range(PAIRS):
            a = qt[2 * p * HD : (2 * p + 1) * HD, s * blk : (s + 1) * blk]
            b = qt[(2 * p + 1) * HD : (2 * p + 2) * HD, s * blk : (s + 1) * blk]
            qpad[s, p] = jnp.concatenate(
                [jnp.concatenate([a, zero], 1), jnp.concatenate([zero, b], 1)], 0
            )

    def project(rows, put_k, put_v):
        k = dot_nn(rows, w3[1]).astype(BF16)
        v = dot_nt(wvt[...], rows).astype(BF16)
        for i in range(slots):
            put_k(i, k[i * blk : (i + 1) * blk])
            put_v(i, v[:, i * blk : (i + 1) * blk])

    def setter(ref, where):
        def put(i, value):
            ref[where(i)] = value
        return put

    project(own, setter(kown, lambda i: i), setter(vown, lambda i: i))
    near_copy.wait_recv()
    project(near[...], setter(knear, lambda i: i), setter(vnear, lambda i: i))
    for i in (2, 6):
        loads[i].wait()

    def run(units):
        waiting = None
        scores = units[0][0]()
        for i, (_, values, put) in enumerate(units):
            following = units[i + 1][0]() if i + 1 < len(units) else None
            m = functools.reduce(jnp.maximum, [jnp.max(a, 0, keepdims=True) for a in scores])
            expo = [jnp.exp(a - m) for a in scores]
            l = functools.reduce(jnp.add, [jnp.sum(a, 0, keepdims=True) for a in expo])
            expo = [a.astype(BF16) for a in expo]
            if waiting is not None:
                waiting()
            waiting = functools.partial(
                lambda values, put, expo, m, l: put(values(expo), m, l), values, put, expo, m, l
            )
            scores = following
        waiting()

    def keep(o_ref, m_ref, l_ref, at, p, o, m, l):
        o_ref[at + (pl.ds(2 * p * HD, HD),)] = o[:HD, :blk]
        o_ref[at + (pl.ds((2 * p + 1) * HD, HD),)] = o[HD:, blk:]
        for half in range(2):
            cols = slice(half * blk, (half + 1) * blk)
            m_ref[at + (pl.ds(2 * p + half, 1),)] = m[:, cols]
            l_ref[at + (pl.ds(2 * p + half, 1),)] = l[:, cols]

    bit_row = lax.broadcasted_iota(jnp.int32, (16, blk), 0)
    key_at = lax.broadcasted_iota(jnp.int32, (blk, blk), 0)
    query_at = lax.broadcasted_iota(jnp.int32, (blk, blk), 1)
    units = []
    for s in range(slots):
        words = pat[s]
        picked = jnp.concatenate(
            [
                jnp.right_shift(jnp.broadcast_to(words[w : w + 1], (16, blk)), bit_row) & 1
                for w in range(blk // 16)
            ],
            0,
        )
        bias = jnp.where((picked == 1) | (key_at == query_at), 0.0, -1e30).astype(F32)
        bias = jnp.concatenate([bias, bias], 1)
        linked = partner[s, 0]
        k1 = knear[linked]
        v1 = vnear[linked]
        for p in range(PAIRS):
            cols = slice(2 * p * HD, 2 * (p + 1) * HD)

            def scores(s=s, p=p, cols=cols, bias=bias, k1=k1):
                q = qpad[s, p]
                return [dot_nn(kown[s, :, cols], q) + bias, dot_nn(k1[:, cols], q)]

            def values(e, s=s, cols=cols, v1=v1):
                return dot_nn(
                    jnp.concatenate([vown[s, cols], v1[cols]], 1), jnp.concatenate(e, 0)
                )

            units.append((scores, values, functools.partial(keep, ob, mb, lb, (s,), p)))
    run(units)

    for i in (3, 4, 5):
        loads[i].wait()

    for j in range(2, slots):
        for l in range(LINKS - 1):
            far_copies[j - 2][l].wait_send()
            far_copies[j][l].start()

    ranks, order = [], []
    for l in range(1, LINKS):
        named = [partner[s, l] for s in range(slots)]
        rank = []
        for s in range(slots):
            r = jnp.int32(0)
            for t in range(slots):
                if t != s:
                    before = named[t] <= named[s] if t < s else named[t] < named[s]
                    r = r + jnp.where(before, 1, 0).astype(jnp.int32)
            rank.append(r)
        at = []
        for j in range(slots):
            slot, block = jnp.int32(0), jnp.int32(0)
            for s in range(slots):
                slot = jnp.where(rank[s] == j, s, slot)
                block = jnp.where(rank[s] == j, named[s], block)
            at.append((slot, block))
        ranks.append(rank)
        order.append(at)

    for j in range(slots):
        for l in range(LINKS - 1):
            far_copies[j][l].wait_recv()
        rows = far[j]
        k = dot_nn(rows, w3[1]).astype(BF16)
        v = dot_nt(wvt[...], rows).astype(BF16)
        for l in range(LINKS - 1):
            kfar[l, j] = k[l * blk : (l + 1) * blk]
            vfar[l, j] = v[:, l * blk : (l + 1) * blk]
        units = []
        for l in range(LINKS - 1):
            slot, block = order[l][j]
            for p in range(PAIRS):
                cols = slice(2 * p * HD, 2 * (p + 1) * HD)

                def scores(l=l, slot=slot, block=block, p=p, cols=cols):
                    return [dot_nn(kfar[l, block, :, cols], qpad[slot, p])]

                def values(e, l=l, block=block, cols=cols):
                    return dot_nn(vfar[l, block, cols], e[0])

                units.append((scores, values, functools.partial(keep, of, mf, lf, (l, j), p)))
        run(units)

    for s in range(slots):
        ms = [mb[s]] + [mf[l, ranks[l][s]] for l in range(LINKS - 1)]
        ls = [lb[s]] + [lf[l, ranks[l][s]] for l in range(LINKS - 1)]
        os = [ob[s]] + [of[l, ranks[l][s]] for l in range(LINKS - 1)]
        top = functools.reduce(jnp.maximum, ms)
        scale = [jnp.exp(m - top) for m in ms]
        total = functools.reduce(jnp.add, [a * b for a, b in zip(scale, ls)])
        scale = [a / total for a in scale]
        heads = []
        for h in range(H):
            heads.append(functools.reduce(
                jnp.add,
                [o[h * HD : (h + 1) * HD] * a[h : h + 1] for o, a in zip(os, scale)],
            ))
        joined = jnp.concatenate(heads, 0)
        here = pl.ds(s * blk, blk)
        resid = x[here].astype(F32) + dot_nn(joined.astype(BF16).T, wo[...])
        mean = jnp.mean(resid, 1, keepdims=True)
        var = jnp.mean(resid * resid, 1, keepdims=True) - mean * mean
        normed = (resid - mean) * lax.rsqrt(var + epsilon)
        nf[here] = normed
        nb[here] = normed.astype(BF16)

    hidden = jnp.maximum(dot_nn(nb[...], wu[...]), 0.0).astype(BF16)
    mixed = nf[...] + dot_nn(hidden, wd[...])
    live = counts[0]
    for s in range(slots):
        part = mixed[s * blk : (s + 1) * blk]
        out_ref[pl.ds(s * blk, blk)] = jnp.where(s < live, part, 0.0).astype(BF16)

    near_copy.wait_send()
    for row in far_copies[max(slots - 2, 0):]:
        for copy in row:
            copy.wait_send()


def local(features, w_qkv, w_out, w_up, w_down, pattern, partner, counts):
    rows, width = features.shape
    slots = partner.shape[0]
    blk = rows // slots
    ff = w_up.shape[1]
    words = pattern.shape[2]
    log_size = (lax.axis_size("nodes") * lax.axis_size("heads")).bit_length() - 1
    bits = [i * log_size // 4 for i in range(LINKS)]
    far = LINKS - 1
    any_spec = pl.BlockSpec(memory_space=pl.ANY)
    vm = pltpu.VMEM
    sem = pltpu.SemaphoreType.DMA
    operands = [
        pltpu.with_memory_space_constraint(a, pltpu.HBM)
        for a in (
            features, jnp.transpose(w_qkv, (1, 0, 2)), w_out, w_up, w_down,
            jnp.transpose(pattern, (0, 2, 1)), partner,
        )
    ]
    return pl.pallas_call(
        functools.partial(kernel, bits, slots, blk),
        out_shape=pltpu.VMEM((rows, width), BF16),
        in_specs=[any_spec] * 7 + [pl.BlockSpec(memory_space=pltpu.SMEM)],
        out_specs=pl.BlockSpec(memory_space=pltpu.VMEM),
        scratch_shapes=[
            pltpu.SMEM(partner.shape, jnp.int32),
            vm((rows, width), BF16),
            vm((3, width, width), BF16),
            vm((width, width), BF16),
            vm((width, ff), BF16),
            vm((ff, width), BF16),
            vm((slots, words, blk), jnp.int32),
            vm((width, width), BF16),
            vm((width, width), BF16),
            vm((rows, width), BF16),
            vm((slots, far * blk, width), BF16),
            vm((slots, PAIRS, 2 * HD, 2 * blk), BF16),
            vm((slots, blk, width), BF16),
            vm((slots, width, blk), BF16),
            vm((slots, blk, width), BF16),
            vm((slots, width, blk), BF16),
            vm((far, slots, blk, width), BF16),
            vm((far, slots, width, blk), BF16),
            vm((slots, width, blk), F32),
            vm((slots, H, blk), F32),
            vm((slots, H, blk), F32),
            vm((far, slots, width, blk), F32),
            vm((far, slots, H, blk), F32),
            vm((far, slots, H, blk), F32),
            vm((rows, width), F32),
            vm((rows, width), BF16),
            sem((7,)),
            sem,
            sem,
            sem((slots, far)),
            sem((slots, far)),
        ],
        compiler_params=pltpu.CompilerParams(
            collective_id=0, has_side_effects=True, vmem_limit_bytes=48 * 2**20
        ),
        cost_estimate=pl.CostEstimate(
            flops=5 * 10**9, bytes_accessed=10 * 2**20, transcendentals=2 * 10**6
        ),
        name="layer",
    )(*operands, counts)


def solution(mesh):
    placed = (
        P(("nodes", "heads"), None),
        P(),
        P(),
        P(),
        P(),
        P(("nodes", "heads"), None, None),
        P(("nodes", "heads"), None),
        P(("nodes", "heads")),
    )
    return jax.shard_map(
        local, mesh=mesh, in_specs=placed, out_specs=P(("nodes", "heads"), None), check_vma=False
    )
```

```python
import functools

import jax
import jax.numpy as jnp
from jax import lax
from jax.experimental import pallas as pl
from jax.experimental.pallas import tpu as pltpu
from jax.sharding import PartitionSpec as P

D = 512
H = 8
HD = D // H
PAIRS = H // 2
LINKS = 4

epsilon = 1e-05
F32 = jnp.float32
BF16 = jnp.bfloat16


def flip(index, mask):
    return index + mask - 2 * mask * ((index // mask) % 2)


def dot_nn(a, b):
    return jnp.dot(a, b, preferred_element_type=F32)


def dot_nt(a, b):
    return lax.dot_general(a, b, (((1,), (1,)), ((), ())), preferred_element_type=F32)


def kernel(
    bits, slots, blk,
    feat_hbm, w3_hbm, wo_hbm, wu_hbm, wd_hbm, pat_hbm, partner_hbm, counts,
    out_ref,
    partner, x, w3, wo, wu, wd, pat, wqt, wvt, near, far,
    qpad, kown, vown, knear, vnear, kfar, vfar,
    ob, mb, lb, of, mf, lf, nf, nb,
    load_sem, near_send, near_recv, far_send, far_recv,
):
    node = lax.axis_index("nodes")
    core = lax.axis_index("heads")

    def target(bit):
        if bit == 0:
            return (node, flip(core, 1))
        return (flip(node, 2 ** (bit - 1)), core)

    loads = []
    for i, (src, dst) in enumerate(
        [(w3_hbm, w3), (feat_hbm, x), (pat_hbm, pat), (wo_hbm, wo), (wu_hbm, wu), (wd_hbm, wd),
         (partner_hbm, partner)]
    ):
        loads.append(pltpu.make_async_copy(src, dst, load_sem.at[i]))
        loads[-1].start()

    barrier = pltpu.get_barrier_semaphore()
    for bit in bits:
        pl.semaphore_signal(
            barrier, inc=1, device_id=target(bit), device_id_type=pl.DeviceIdType.MESH
        )
    pl.semaphore_wait(barrier, LINKS)

    far_copies = []
    near_copy = pltpu.make_async_remote_copy(
        src_ref=feat_hbm, dst_ref=near, send_sem=near_send, recv_sem=near_recv,
        device_id=target(bits[0]), device_id_type=pl.DeviceIdType.MESH,
    )
    for j in range(slots):
        row = []
        for l in range(LINKS - 1):
            row.append(pltpu.make_async_remote_copy(
                src_ref=feat_hbm.at[pl.ds(j * blk, blk)],
                dst_ref=far.at[j, pl.ds(l * blk, blk)],
                send_sem=far_send.at[j, l], recv_sem=far_recv.at[j, l],
                device_id=target(bits[l + 1]), device_id_type=pl.DeviceIdType.MESH,
            ))
            if j < 2:
                row[-1].start()
        far_copies.append(row)
        if j == 0:
            near_copy.start()

    loads[0].wait()
    loads[1].wait()
    wqt[...] = w3[0].T
    wvt[...] = w3[2].T
    own = x[...]
    qt = dot_nt(wqt[...], own).astype(BF16) * jnp.asarray(1.0 / HD**0.5, BF16)
    zero = jnp.zeros((HD, blk), BF16)
    for s in range(slots):
        for p in range(PAIRS):
            a = qt[2 * p * HD : (2 * p + 1) * HD, s * blk : (s + 1) * blk]
            b = qt[(2 * p + 1) * HD : (2 * p + 2) * HD, s * blk : (s + 1) * blk]
            qpad[s, p] = jnp.concatenate(
                [jnp.concatenate([a, zero], 1), jnp.concatenate([zero, b], 1)], 0
            )
    near_copy.wait_recv()
    both = jnp.concatenate([own, near[...]], 0)
    k = dot_nn(both, w3[1]).astype(BF16)
    v = dot_nt(wvt[...], both).astype(BF16)
    for i in range(slots):
        kown[i] = k[i * blk : (i + 1) * blk]
        vown[i] = v[:, i * blk : (i + 1) * blk]
        knear[i] = k[(slots + i) * blk : (slots + i + 1) * blk]
        vnear[i] = v[:, (slots + i) * blk : (slots + i + 1) * blk]
    for i in (2, 6):
        loads[i].wait()

    def run(units):
        waiting = None
        scores = units[0][0]()
        for i, (_, values, put) in enumerate(units):
            following = units[i + 1][0]() if i + 1 < len(units) else None
            m = functools.reduce(jnp.maximum, [jnp.max(a, 0, keepdims=True) for a in scores])
            expo = [jnp.exp(a - m) for a in scores]
            l = functools.reduce(jnp.add, [jnp.sum(a, 0, keepdims=True) for a in expo])
            expo = [a.astype(BF16) for a in expo]
            if waiting is not None:
                waiting()
            waiting = functools.partial(
                lambda values, put, expo, m, l: put(values(expo), m, l), values, put, expo, m, l
            )
            scores = following
        waiting()

    def keep(o_ref, m_ref, l_ref, at, p, o, m, l):
        o_ref[at + (pl.ds(2 * p * HD, HD),)] = o[:HD, :blk]
        o_ref[at + (pl.ds((2 * p + 1) * HD, HD),)] = o[HD:, blk:]
        for half in range(2):
            cols = slice(half * blk, (half + 1) * blk)
            m_ref[at + (pl.ds(2 * p + half, 1),)] = m[:, cols]
            l_ref[at + (pl.ds(2 * p + half, 1),)] = l[:, cols]

    bit_row = lax.broadcasted_iota(jnp.int32, (16, blk), 0)
    key_at = lax.broadcasted_iota(jnp.int32, (blk, blk), 0)
    query_at = lax.broadcasted_iota(jnp.int32, (blk, blk), 1)
    units = []
    for s in range(slots):
        words = pat[s]
        picked = jnp.concatenate(
            [
                jnp.right_shift(jnp.broadcast_to(words[w : w + 1], (16, blk)), bit_row) & 1
                for w in range(blk // 16)
            ],
            0,
        )
        bias = jnp.where((picked == 1) | (key_at == query_at), 0.0, -1e30).astype(F32)
        bias = jnp.concatenate([bias, bias], 1)
        linked = partner[s, 0]
        k1 = knear[linked]
        v1 = vnear[linked]
        for p in range(PAIRS):
            cols = slice(2 * p * HD, 2 * (p + 1) * HD)

            def scores(s=s, p=p, cols=cols, bias=bias, k1=k1):
                both = dot_nn(jnp.concatenate([kown[s, :, cols], k1[:, cols]], 0), qpad[s, p])
                return [both[:blk] + bias, both[blk:]]

            def values(e, s=s, cols=cols, v1=v1):
                return dot_nn(
                    jnp.concatenate([vown[s, cols], v1[cols]], 1), jnp.concatenate(e, 0)
                )

            units.append((scores, values, functools.partial(keep, ob, mb, lb, (s,), p)))
    run(units)

    for i in (3, 4, 5):
        loads[i].wait()

    for j in range(2, slots):
        for l in range(LINKS - 1):
            far_copies[j - 2][l].wait_send()
            far_copies[j][l].start()

    ranks, order = [], []
    for l in range(1, LINKS):
        named = [partner[s, l] for s in range(slots)]
        rank = []
        for s in range(slots):
            r = jnp.int32(0)
            for t in range(slots):
                if t != s:
                    before = named[t] <= named[s] if t < s else named[t] < named[s]
                    r = r + jnp.where(before, 1, 0).astype(jnp.int32)
            rank.append(r)
        at = []
        for j in range(slots):
            slot, block = jnp.int32(0), jnp.int32(0)
            for s in range(slots):
                slot = jnp.where(rank[s] == j, s, slot)
                block = jnp.where(rank[s] == j, named[s], block)
            at.append((slot, block))
        ranks.append(rank)
        order.append(at)

    for j in range(slots):
        for l in range(LINKS - 1):
            far_copies[j][l].wait_recv()
        rows = far[j]
        k = dot_nn(rows, w3[1]).astype(BF16)
        v = dot_nt(wvt[...], rows).astype(BF16)
        for l in range(LINKS - 1):
            kfar[l, j] = k[l * blk : (l + 1) * blk]
            vfar[l, j] = v[:, l * blk : (l + 1) * blk]
        units = []
        for l in range(LINKS - 1):
            slot, block = order[l][j]
            for p in range(PAIRS):
                cols = slice(2 * p * HD, 2 * (p + 1) * HD)

                def scores(l=l, slot=slot, block=block, p=p, cols=cols):
                    return [dot_nn(kfar[l, block, :, cols], qpad[slot, p])]

                def values(e, l=l, block=block, cols=cols):
                    return dot_nn(vfar[l, block, cols], e[0])

                units.append((scores, values, functools.partial(keep, of, mf, lf, (l, j), p)))
        run(units)

    for s in range(slots):
        ms = [mb[s]] + [mf[l, ranks[l][s]] for l in range(LINKS - 1)]
        ls = [lb[s]] + [lf[l, ranks[l][s]] for l in range(LINKS - 1)]
        os = [ob[s]] + [of[l, ranks[l][s]] for l in range(LINKS - 1)]
        top = functools.reduce(jnp.maximum, ms)
        scale = [jnp.exp(m - top) for m in ms]
        total = functools.reduce(jnp.add, [a * b for a, b in zip(scale, ls)])
        scale = [a / total for a in scale]
        heads = []
        for h in range(H):
            heads.append(functools.reduce(
                jnp.add,
                [o[h * HD : (h + 1) * HD] * a[h : h + 1] for o, a in zip(os, scale)],
            ))
        joined = jnp.concatenate(heads, 0)
        here = pl.ds(s * blk, blk)
        resid = x[here].astype(F32) + dot_nn(joined.astype(BF16).T, wo[...])
        mean = jnp.mean(resid, 1, keepdims=True)
        var = jnp.mean(resid * resid, 1, keepdims=True) - mean * mean
        normed = (resid - mean) * lax.rsqrt(var + epsilon)
        nf[here] = normed
        nb[here] = normed.astype(BF16)

    hidden = jnp.maximum(dot_nn(nb[...], wu[...]), 0.0).astype(BF16)
    mixed = nf[...] + dot_nn(hidden, wd[...])
    live = counts[0]
    for s in range(slots):
        part = mixed[s * blk : (s + 1) * blk]
        out_ref[pl.ds(s * blk, blk)] = jnp.where(s < live, part, 0.0).astype(BF16)

    near_copy.wait_send()
    for row in far_copies[max(slots - 2, 0):]:
        for copy in row:
            copy.wait_send()


def local(features, w_qkv, w_out, w_up, w_down, pattern, partner, counts):
    rows, width = features.shape
    slots = partner.shape[0]
    blk = rows // slots
    ff = w_up.shape[1]
    words = pattern.shape[2]
    log_size = (lax.axis_size("nodes") * lax.axis_size("heads")).bit_length() - 1
    bits = [i * log_size // 4 for i in range(LINKS)]
    far = LINKS - 1
    any_spec = pl.BlockSpec(memory_space=pl.ANY)
    vm = pltpu.VMEM
    sem = pltpu.SemaphoreType.DMA
    operands = [
        pltpu.with_memory_space_constraint(a, pltpu.HBM)
        for a in (
            features, jnp.transpose(w_qkv, (1, 0, 2)), w_out, w_up, w_down,
            jnp.transpose(pattern, (0, 2, 1)), partner,
        )
    ]
    return pl.pallas_call(
        functools.partial(kernel, bits, slots, blk),
        out_shape=pltpu.VMEM((rows, width), BF16),
        in_specs=[any_spec] * 7 + [pl.BlockSpec(memory_space=pltpu.SMEM)],
        out_specs=pl.BlockSpec(memory_space=pltpu.VMEM),
        scratch_shapes=[
            pltpu.SMEM(partner.shape, jnp.int32),
            vm((rows, width), BF16),
            vm((3, width, width), BF16),
            vm((width, width), BF16),
            vm((width, ff), BF16),
            vm((ff, width), BF16),
            vm((slots, words, blk), jnp.int32),
            vm((width, width), BF16),
            vm((width, width), BF16),
            vm((rows, width), BF16),
            vm((slots, far * blk, width), BF16),
            vm((slots, PAIRS, 2 * HD, 2 * blk), BF16),
            vm((slots, blk, width), BF16),
            vm((slots, width, blk), BF16),
            vm((slots, blk, width), BF16),
            vm((slots, width, blk), BF16),
            vm((far, slots, blk, width), BF16),
            vm((far, slots, width, blk), BF16),
            vm((slots, width, blk), F32),
            vm((slots, H, blk), F32),
            vm((slots, H, blk), F32),
            vm((far, slots, width, blk), F32),
            vm((far, slots, H, blk), F32),
            vm((far, slots, H, blk), F32),
            vm((rows, width), F32),
            vm((rows, width), BF16),
            sem((7,)),
            sem,
            sem,
            sem((slots, far)),
            sem((slots, far)),
        ],
        compiler_params=pltpu.CompilerParams(
            collective_id=0, has_side_effects=True, vmem_limit_bytes=48 * 2**20
        ),
        cost_estimate=pl.CostEstimate(
            flops=5 * 10**9, bytes_accessed=10 * 2**20, transcendentals=2 * 10**6
        ),
        name="layer",
    )(*operands, counts)


def solution(mesh):
    placed = (
        P(("nodes", "heads"), None),
        P(),
        P(),
        P(),
        P(),
        P(("nodes", "heads"), None, None),
        P(("nodes", "heads"), None),
        P(("nodes", "heads")),
    )
    return jax.shard_map(
        local, mesh=mesh, in_specs=placed, out_specs=P(("nodes", "heads"), None), check_vma=False
    )
```

```python
import functools

import jax
import jax.numpy as jnp
from jax import lax
from jax.experimental import pallas as pl
from jax.experimental.pallas import tpu as pltpu
from jax.sharding import PartitionSpec as P

D = 512
H = 8
HD = D // H
PAIRS = H // 2
LINKS = 4

epsilon = 1e-05
F32 = jnp.float32
BF16 = jnp.bfloat16


def flip(index, mask):
    return index + mask - 2 * mask * ((index // mask) % 2)


def dot_nn(a, b):
    return jnp.dot(a, b, preferred_element_type=F32)


def dot_nt(a, b):
    return lax.dot_general(a, b, (((1,), (1,)), ((), ())), preferred_element_type=F32)


def kernel(
    bits, slots, blk,
    feat_hbm, w3_hbm, wo_hbm, wu_hbm, wd_hbm, pat_hbm, partner_hbm, counts,
    out_ref,
    partner, x, w3, wo, wu, wd, pat, wqt, wvt, near, far,
    qpad, kown, vown, knear, vnear, kfar, vfar,
    ob, mb, lb, of, mf, lf, nf, nb,
    load_sem, near_send, near_recv, far_send, far_recv,
):
    node = lax.axis_index("nodes")
    core = lax.axis_index("heads")

    def target(bit):
        if bit == 0:
            return (node, flip(core, 1))
        return (flip(node, 2 ** (bit - 1)), core)

    barrier = pltpu.get_barrier_semaphore()
    for bit in bits:
        pl.semaphore_signal(
            barrier, inc=1, device_id=target(bit), device_id_type=pl.DeviceIdType.MESH
        )
    loads = []
    for i, (src, dst) in enumerate(
        [(w3_hbm, w3), (feat_hbm, x), (pat_hbm, pat), (wo_hbm, wo), (wu_hbm, wu), (wd_hbm, wd),
         (partner_hbm, partner)]
    ):
        loads.append(pltpu.make_async_copy(src, dst, load_sem.at[i]))
        loads[-1].start()

    pl.semaphore_wait(barrier, LINKS)

    far_copies = []
    near_copy = pltpu.make_async_remote_copy(
        src_ref=feat_hbm, dst_ref=near, send_sem=near_send, recv_sem=near_recv,
        device_id=target(bits[0]), device_id_type=pl.DeviceIdType.MESH,
    )
    half = blk // 2
    pieces = [(j, 0, blk) for j in range(slots - 1)]
    pieces += [(slots - 1, 0, half), (slots - 1, half, half)]
    for n, (j, start, size) in enumerate(pieces):
        row = []
        for l in range(LINKS - 1):
            row.append(pltpu.make_async_remote_copy(
                src_ref=feat_hbm.at[pl.ds(j * blk + start, size)],
                dst_ref=far.at[j, pl.ds((LINKS - 1) * start + l * size, size)],
                send_sem=far_send.at[n, l], recv_sem=far_recv.at[n, l],
                device_id=target(bits[l + 1]), device_id_type=pl.DeviceIdType.MESH,
            ))
            row[-1].start()
        far_copies.append(row)
        if n == 0:
            near_copy.start()

    loads[0].wait()
    loads[1].wait()
    wqt[...] = w3[0].T
    wvt[...] = w3[2].T
    own = x[...]
    qt = dot_nt(wqt[...], own).astype(BF16) * jnp.asarray(1.0 / HD**0.5, BF16)
    zero = jnp.zeros((HD, blk), BF16)
    for s in range(slots):
        for p in range(PAIRS):
            a = qt[2 * p * HD : (2 * p + 1) * HD, s * blk : (s + 1) * blk]
            b = qt[(2 * p + 1) * HD : (2 * p + 2) * HD, s * blk : (s + 1) * blk]
            qpad[s, p] = jnp.concatenate(
                [jnp.concatenate([a, zero], 1), jnp.concatenate([zero, b], 1)], 0
            )
    def project(rows, k_ref, v_ref):
        k = dot_nn(rows, w3[1]).astype(BF16)
        v = dot_nt(wvt[...], rows).astype(BF16)
        for i in range(slots):
            k_ref[i] = k[i * blk : (i + 1) * blk]
            v_ref[i] = v[:, i * blk : (i + 1) * blk]

    project(own, kown, vown)
    near_copy.wait_recv()
    project(near[...], knear, vnear)
    for i in (2, 6):
        loads[i].wait()

    def run(units):
        waiting = None
        scores = units[0][0]()
        for i, (_, values, put) in enumerate(units):
            following = units[i + 1][0]() if i + 1 < len(units) else None
            m = functools.reduce(jnp.maximum, [jnp.max(a, 0, keepdims=True) for a in scores])
            expo = [jnp.exp(a - m) for a in scores]
            l = functools.reduce(jnp.add, [jnp.sum(a, 0, keepdims=True) for a in expo])
            expo = [a.astype(BF16) for a in expo]
            if waiting is not None:
                waiting()
            waiting = functools.partial(
                lambda values, put, expo, m, l: put(values(expo), m, l), values, put, expo, m, l
            )
            scores = following
        waiting()

    def keep(o_ref, m_ref, l_ref, at, p, o, m, l):
        o_ref[at + (pl.ds(2 * p * HD, HD),)] = o[:HD, :blk]
        o_ref[at + (pl.ds((2 * p + 1) * HD, HD),)] = o[HD:, blk:]
        for half in range(2):
            cols = slice(half * blk, (half + 1) * blk)
            m_ref[at + (pl.ds(2 * p + half, 1),)] = m[:, cols]
            l_ref[at + (pl.ds(2 * p + half, 1),)] = l[:, cols]

    bit_row = lax.broadcasted_iota(jnp.int32, (16, blk), 0)
    key_at = lax.broadcasted_iota(jnp.int32, (blk, blk), 0)
    query_at = lax.broadcasted_iota(jnp.int32, (blk, blk), 1)
    units = []
    for s in range(slots):
        words = pat[s]
        picked = jnp.concatenate(
            [
                jnp.right_shift(jnp.broadcast_to(words[w : w + 1], (16, blk)), bit_row) & 1
                for w in range(blk // 16)
            ],
            0,
        )
        bias = jnp.where((picked == 1) | (key_at == query_at), 0.0, -1e30).astype(F32)
        bias = jnp.concatenate([bias, bias], 1)
        linked = partner[s, 0]
        k1 = knear[linked]
        v1 = vnear[linked]
        for p in range(PAIRS):
            cols = slice(2 * p * HD, 2 * (p + 1) * HD)

            def scores(s=s, p=p, cols=cols, bias=bias, k1=k1):
                both = dot_nn(jnp.concatenate([kown[s, :, cols], k1[:, cols]], 0), qpad[s, p])
                return [both[:blk] + bias, both[blk:]]

            def values(e, s=s, cols=cols, v1=v1):
                return dot_nn(
                    jnp.concatenate([vown[s, cols], v1[cols]], 1), jnp.concatenate(e, 0)
                )

            units.append((scores, values, functools.partial(keep, ob, mb, lb, (s,), p)))
    run(units)

    for i in (3, 4, 5):
        loads[i].wait()

    ranks, order = [], []
    for l in range(1, LINKS):
        named = [partner[s, l] for s in range(slots)]
        rank = []
        for s in range(slots):
            r = jnp.int32(0)
            for t in range(slots):
                if t != s:
                    before = named[t] <= named[s] if t < s else named[t] < named[s]
                    r = r + jnp.where(before, 1, 0).astype(jnp.int32)
            rank.append(r)
        at = []
        for j in range(slots):
            slot, block = jnp.int32(0), jnp.int32(0)
            for s in range(slots):
                slot = jnp.where(rank[s] == j, s, slot)
                block = jnp.where(rank[s] == j, named[s], block)
            at.append((slot, block))
        ranks.append(rank)
        order.append(at)

    def merge(o_ref, m_ref, l_ref, at, p, o, m, l):
        for side in range(2):
            h = 2 * p + side
            cols = slice(side * blk, (side + 1) * blk)
            rows = at + (pl.ds(h * HD, HD),)
            row = at + (pl.ds(h, 1),)
            before = m_ref[row]
            top = jnp.maximum(before, m[:, cols])
            old, new = jnp.exp(before - top), jnp.exp(m[:, cols] - top)
            o_ref[rows] = o_ref[rows] * old + o[side * HD : (side + 1) * HD, cols] * new
            l_ref[row] = l_ref[row] * old + l[:, cols] * new
            m_ref[row] = top

    for n, (j, start, size) in enumerate(pieces):
        for l in range(LINKS - 1):
            far_copies[n][l].wait_recv()
        rows = far[j, pl.ds((LINKS - 1) * start, (LINKS - 1) * size)]
        k = dot_nn(rows, w3[1]).astype(BF16)
        v = dot_nt(wvt[...], rows).astype(BF16)
        for l in range(LINKS - 1):
            vl = v[:, l * size : (l + 1) * size]
            kfar[l, j, pl.ds(start, size)] = k[l * size : (l + 1) * size]
            if size < blk and start == 0:
                vl = jnp.concatenate([vl, jnp.zeros((D, blk - size), BF16)], 1)
                vfar[l, j] = vl
            else:
                vfar[l, j, :, pl.ds(start, size)] = vl
        units = []
        for l in range(LINKS - 1):
            slot, block = order[l][j]
            for p in range(PAIRS):
                cols = slice(2 * p * HD, 2 * (p + 1) * HD)

                def scores(l=l, slot=slot, block=block, p=p, cols=cols, rows=pl.ds(start, size)):
                    return [dot_nn(kfar[l, block, rows, cols], qpad[slot, p])]

                def values(e, l=l, block=block, cols=cols, start=start, size=size):
                    parts = [e[0]]
                    if size < blk:
                        rest = jnp.zeros((blk - size, 2 * blk), BF16)
                        parts = [rest] + parts if start else parts + [rest]
                    return dot_nn(vfar[l, block, cols], jnp.concatenate(parts, 0))

                put = merge if start else keep
                units.append((scores, values, functools.partial(put, of, mf, lf, (l, j), p)))
        run(units)

    for s in range(slots):
        ms = [mb[s]] + [mf[l, ranks[l][s]] for l in range(LINKS - 1)]
        ls = [lb[s]] + [lf[l, ranks[l][s]] for l in range(LINKS - 1)]
        os = [ob[s]] + [of[l, ranks[l][s]] for l in range(LINKS - 1)]
        top = functools.reduce(jnp.maximum, ms)
        scale = [jnp.exp(m - top) for m in ms]
        total = functools.reduce(jnp.add, [a * b for a, b in zip(scale, ls)])
        scale = [a / total for a in scale]
        heads = []
        for h in range(H):
            heads.append(functools.reduce(
                jnp.add,
                [o[h * HD : (h + 1) * HD] * a[h : h + 1] for o, a in zip(os, scale)],
            ))
        joined = jnp.concatenate(heads, 0)
        here = pl.ds(s * blk, blk)
        resid = x[here].astype(F32) + dot_nn(joined.astype(BF16).T, wo[...])
        mean = jnp.mean(resid, 1, keepdims=True)
        var = jnp.mean(resid * resid, 1, keepdims=True) - mean * mean
        normed = (resid - mean) * lax.rsqrt(var + epsilon)
        nf[here] = normed
        nb[here] = normed.astype(BF16)

    hidden = jnp.maximum(dot_nn(nb[...], wu[...]), 0.0).astype(BF16)
    mixed = nf[...] + dot_nn(hidden, wd[...])
    live = counts[0]
    for s in range(slots):
        part = mixed[s * blk : (s + 1) * blk]
        out_ref[pl.ds(s * blk, blk)] = jnp.where(s < live, part, 0.0).astype(BF16)

    near_copy.wait_send()
    for row in far_copies:
        for copy in row:
            copy.wait_send()


def local(features, w_qkv, w_out, w_up, w_down, pattern, partner, counts):
    rows, width = features.shape
    slots = partner.shape[0]
    blk = rows // slots
    ff = w_up.shape[1]
    words = pattern.shape[2]
    log_size = (lax.axis_size("nodes") * lax.axis_size("heads")).bit_length() - 1
    bits = [i * log_size // 4 for i in range(LINKS)]
    far = LINKS - 1
    any_spec = pl.BlockSpec(memory_space=pl.ANY)
    vm = pltpu.VMEM
    sem = pltpu.SemaphoreType.DMA
    operands = [
        pltpu.with_memory_space_constraint(a, pltpu.HBM)
        for a in (
            features, jnp.transpose(w_qkv, (1, 0, 2)), w_out, w_up, w_down,
            jnp.transpose(pattern, (0, 2, 1)), partner,
        )
    ]
    return pl.pallas_call(
        functools.partial(kernel, bits, slots, blk),
        out_shape=pltpu.VMEM((rows, width), BF16),
        in_specs=[any_spec] * 7 + [pl.BlockSpec(memory_space=pltpu.SMEM)],
        out_specs=pl.BlockSpec(memory_space=pltpu.VMEM),
        scratch_shapes=[
            pltpu.SMEM(partner.shape, jnp.int32),
            vm((rows, width), BF16),
            vm((3, width, width), BF16),
            vm((width, width), BF16),
            vm((width, ff), BF16),
            vm((ff, width), BF16),
            vm((slots, words, blk), jnp.int32),
            vm((width, width), BF16),
            vm((width, width), BF16),
            vm((rows, width), BF16),
            vm((slots, far * blk, width), BF16),
            vm((slots, PAIRS, 2 * HD, 2 * blk), BF16),
            vm((slots, blk, width), BF16),
            vm((slots, width, blk), BF16),
            vm((slots, blk, width), BF16),
            vm((slots, width, blk), BF16),
            vm((far, slots, blk, width), BF16),
            vm((far, slots, width, blk), BF16),
            vm((slots, width, blk), F32),
            vm((slots, H, blk), F32),
            vm((slots, H, blk), F32),
            vm((far, slots, width, blk), F32),
            vm((far, slots, H, blk), F32),
            vm((far, slots, H, blk), F32),
            vm((rows, width), F32),
            vm((rows, width), BF16),
            sem((7,)),
            sem,
            sem,
            sem((slots + 1, far)),
            sem((slots + 1, far)),
        ],
        compiler_params=pltpu.CompilerParams(
            collective_id=0, has_side_effects=True, vmem_limit_bytes=48 * 2**20
        ),
        cost_estimate=pl.CostEstimate(
            flops=5 * 10**9, bytes_accessed=10 * 2**20, transcendentals=2 * 10**6
        ),
        name="layer",
    )(*operands, counts)


def solution(mesh):
    placed = (
        P(("nodes", "heads"), None),
        P(),
        P(),
        P(),
        P(),
        P(("nodes", "heads"), None, None),
        P(("nodes", "heads"), None),
        P(("nodes", "heads")),
    )
    return jax.shard_map(
        local, mesh=mesh, in_specs=placed, out_specs=P(("nodes", "heads"), None), check_vma=False
    )
```

```python
import functools

import jax
import jax.numpy as jnp
from jax import lax
from jax.experimental import pallas as pl
from jax.experimental.pallas import tpu as pltpu
from jax.sharding import PartitionSpec as P

D = 512
H = 8
HD = D // H
PAIRS = H // 2
LINKS = 4

epsilon = 1e-05
F32 = jnp.float32
BF16 = jnp.bfloat16


def flip(index, mask):
    return index + mask - 2 * mask * ((index // mask) % 2)


def dot_nn(a, b):
    return jnp.dot(a, b, preferred_element_type=F32)


def dot_nt(a, b):
    return lax.dot_general(a, b, (((1,), (1,)), ((), ())), preferred_element_type=F32)


def kernel(
    bits, slots, blk,
    feat_hbm, w3_hbm, wo_hbm, wu_hbm, wd_hbm, pat_hbm, partner_hbm, counts,
    out_ref,
    partner, x, w3, wo, wu, wd, pat, wqt, wvt, near, far,
    qpad, kown, vown, knear, vnear, kfar, vfar,
    ob, mb, lb, of, mf, lf, nb,
    load_sem, near_send, near_recv, far_send, far_recv,
):
    node = lax.axis_index("nodes")
    core = lax.axis_index("heads")

    def target(bit):
        if bit == 0:
            return (node, flip(core, 1))
        return (flip(node, 2 ** (bit - 1)), core)

    barrier = pltpu.get_barrier_semaphore()
    for bit in bits:
        pl.semaphore_signal(
            barrier, inc=1, device_id=target(bit), device_id_type=pl.DeviceIdType.MESH
        )
    loads = []
    for i, (src, dst) in enumerate(
        [(w3_hbm, w3), (feat_hbm, x), (pat_hbm, pat), (wo_hbm, wo), (wu_hbm, wu), (wd_hbm, wd),
         (partner_hbm, partner)]
    ):
        loads.append(pltpu.make_async_copy(src, dst, load_sem.at[i]))
        loads[-1].start()

    pl.semaphore_wait(barrier, LINKS)

    def far_copy(j, l):
        return pltpu.make_async_remote_copy(
            src_ref=feat_hbm.at[pl.ds(pl.multiple_of(j * blk, blk), blk)],
            dst_ref=far.at[j, pl.ds(l * blk, blk)],
            send_sem=far_send.at[j, l], recv_sem=far_recv.at[j, l],
            device_id=target(bits[l + 1]), device_id_type=pl.DeviceIdType.MESH,
        )

    near_copy = pltpu.make_async_remote_copy(
        src_ref=feat_hbm, dst_ref=near, send_sem=near_send, recv_sem=near_recv,
        device_id=target(bits[0]), device_id_type=pl.DeviceIdType.MESH,
    )
    for j in range(slots):
        for l in range(LINKS - 1):
            far_copy(j, l).start()
        if j == 0:
            near_copy.start()

    loads[0].wait()
    loads[1].wait()
    wqt[...] = w3[0].T
    wvt[...] = w3[2].T
    own = x[...]
    qt = dot_nt(wqt[...], own).astype(BF16) * jnp.asarray(1.0 / HD**0.5, BF16)
    zero = jnp.zeros((HD, blk), BF16)
    for s in range(slots):
        for p in range(PAIRS):
            a = qt[2 * p * HD : (2 * p + 1) * HD, s * blk : (s + 1) * blk]
            b = qt[(2 * p + 1) * HD : (2 * p + 2) * HD, s * blk : (s + 1) * blk]
            qpad[s, p] = jnp.concatenate(
                [jnp.concatenate([a, zero], 1), jnp.concatenate([zero, b], 1)], 0
            )

    def project(rows, put_k, put_v):
        k = dot_nn(rows, w3[1]).astype(BF16)
        v = dot_nt(wvt[...], rows).astype(BF16)
        for i in range(slots):
            put_k(i, k[i * blk : (i + 1) * blk])
            put_v(i, v[:, i * blk : (i + 1) * blk])

    def setter(ref, where):
        def put(i, value):
            ref[where(i)] = value
        return put

    project(own, setter(kown, lambda i: i), setter(vown, lambda i: i))
    near_copy.wait_recv()
    project(near[...], setter(knear, lambda i: i), setter(vnear, lambda i: i))
    for i in (2, 6):
        loads[i].wait()

    def run(units):
        waiting = None
        scores = units[0][0]()
        for i, (_, values, put) in enumerate(units):
            following = units[i + 1][0]() if i + 1 < len(units) else None
            m = functools.reduce(jnp.maximum, [jnp.max(a, 0, keepdims=True) for a in scores])
            expo = [jnp.exp(a - m) for a in scores]
            l = functools.reduce(jnp.add, [jnp.sum(a, 0, keepdims=True) for a in expo])
            expo = [a.astype(BF16) for a in expo]
            if waiting is not None:
                waiting()
            waiting = functools.partial(
                lambda values, put, expo, m, l: put(values(expo), m, l), values, put, expo, m, l
            )
            scores = following
        waiting()

    def keep(o_ref, m_ref, l_ref, at, p, o, m, l):
        o_ref[at + (pl.ds(2 * p * HD, HD),)] = o[:HD, :blk]
        o_ref[at + (pl.ds((2 * p + 1) * HD, HD),)] = o[HD:, blk:]
        for half in range(2):
            cols = slice(half * blk, (half + 1) * blk)
            m_ref[at + (pl.ds(2 * p + half, 1),)] = m[:, cols]
            l_ref[at + (pl.ds(2 * p + half, 1),)] = l[:, cols]

    bit_row = lax.broadcasted_iota(jnp.int32, (16, blk), 0)
    key_at = lax.broadcasted_iota(jnp.int32, (blk, blk), 0)
    query_at = lax.broadcasted_iota(jnp.int32, (blk, blk), 1)
    def attend_base(s, carry):
        words = pat[s]
        picked = jnp.concatenate(
            [
                jnp.right_shift(jnp.broadcast_to(words[w : w + 1], (16, blk)), bit_row) & 1
                for w in range(blk // 16)
            ],
            0,
        )
        bias = jnp.where((picked == 1) | (key_at == query_at), 0.0, -1e30).astype(F32)
        bias = jnp.concatenate([bias, bias], 1)
        linked = partner[s, 0]
        units = []
        for p in range(PAIRS):
            cols = slice(2 * p * HD, 2 * (p + 1) * HD)

            def scores(p=p, cols=cols):
                keys = jnp.concatenate([kown[s, :, cols], knear[linked, :, cols]], 0)
                both = dot_nn(keys, qpad[s, p])
                return [both[:blk] + bias, both[blk:]]

            def values(e, cols=cols):
                return dot_nn(
                    jnp.concatenate([vown[s, cols], vnear[linked, cols]], 1),
                    jnp.concatenate(e, 0),
                )

            units.append((scores, values, functools.partial(keep, ob, mb, lb, (s,), p)))
        run(units)
        return carry

    lax.fori_loop(0, slots, attend_base, 0)

    for i in (3, 4, 5):
        loads[i].wait()

    ranks, order = [], []
    for l in range(1, LINKS):
        named = [partner[s, l] for s in range(slots)]
        rank = []
        for s in range(slots):
            r = jnp.int32(0)
            for t in range(slots):
                if t != s:
                    before = named[t] <= named[s] if t < s else named[t] < named[s]
                    r = r + jnp.where(before, 1, 0).astype(jnp.int32)
            rank.append(r)
        at = []
        for j in range(slots):
            slot, block = jnp.int32(0), jnp.int32(0)
            for s in range(slots):
                slot = jnp.where(rank[s] == j, s, slot)
                block = jnp.where(rank[s] == j, named[s], block)
            at.append((slot, block))
        ranks.append(rank)
        order.append(at)

    def pick(j, choices):
        result = choices[-1]
        for i in range(len(choices) - 1):
            result = jnp.where(j == i, choices[i], result)
        return result

    def attend_far(j, carry):
        for l in range(LINKS - 1):
            far_copy(j, l).wait_recv()
        rows = far[j]
        k = dot_nn(rows, w3[1]).astype(BF16)
        v = dot_nt(wvt[...], rows).astype(BF16)
        for l in range(LINKS - 1):
            kfar[l, j] = k[l * blk : (l + 1) * blk]
            vfar[l, j] = v[:, l * blk : (l + 1) * blk]
        units = []
        for l in range(LINKS - 1):
            slot = pick(j, [a for a, _ in order[l]])
            block = pick(j, [a for _, a in order[l]])
            for p in range(PAIRS):
                cols = slice(2 * p * HD, 2 * (p + 1) * HD)

                def scores(l=l, slot=slot, block=block, p=p, cols=cols):
                    return [dot_nn(kfar[l, block, :, cols], qpad[slot, p])]

                def values(e, l=l, block=block, cols=cols):
                    return dot_nn(vfar[l, block, cols], e[0])

                units.append((scores, values, functools.partial(keep, of, mf, lf, (l, j), p)))
        run(units)
        return carry

    lax.fori_loop(0, slots, attend_far, 0)

    def join(s, carry):
        at = [pick(s, ranks[l]) for l in range(LINKS - 1)]
        ms = [mb[s]] + [mf[l, at[l]] for l in range(LINKS - 1)]
        ls = [lb[s]] + [lf[l, at[l]] for l in range(LINKS - 1)]
        top = functools.reduce(jnp.maximum, ms)
        scale = [jnp.exp(m - top) for m in ms]
        total = functools.reduce(jnp.add, [a * b for a, b in zip(scale, ls)])
        scale = [a / total for a in scale]
        heads = []
        for h in range(H):
            rows = pl.ds(h * HD, HD)
            os = [ob[s, rows]] + [of[l, at[l], rows] for l in range(LINKS - 1)]
            heads.append(functools.reduce(
                jnp.add, [o * a[h : h + 1] for o, a in zip(os, scale)]
            ))
        joined = jnp.concatenate(heads, 0).astype(BF16).T
        nb[pl.ds(pl.multiple_of(s * blk, blk), blk)] = joined
        return carry

    lax.fori_loop(0, slots, join, 0)

    resid = x[...].astype(F32) + dot_nn(nb[...], wo[...])
    mean = jnp.mean(resid, 1, keepdims=True)
    var = jnp.mean(resid * resid, 1, keepdims=True) - mean * mean
    normed = (resid - mean) * lax.rsqrt(var + epsilon)
    hidden = jnp.maximum(dot_nn(normed.astype(BF16), wu[...]), 0.0).astype(BF16)
    mixed = normed + dot_nn(hidden, wd[...])
    live = counts[0]
    for s in range(slots):
        part = mixed[s * blk : (s + 1) * blk]
        out_ref[pl.ds(s * blk, blk)] = jnp.where(s < live, part, 0.0).astype(BF16)

    near_copy.wait_send()
    for j in range(slots):
        for l in range(LINKS - 1):
            far_copy(j, l).wait_send()


def local(features, w_qkv, w_out, w_up, w_down, pattern, partner, counts):
    rows, width = features.shape
    slots = partner.shape[0]
    blk = rows // slots
    ff = w_up.shape[1]
    words = pattern.shape[2]
    log_size = (lax.axis_size("nodes") * lax.axis_size("heads")).bit_length() - 1
    bits = [i * log_size // 4 for i in range(LINKS)]
    far = LINKS - 1
    any_spec = pl.BlockSpec(memory_space=pl.ANY)
    vm = pltpu.VMEM
    sem = pltpu.SemaphoreType.DMA
    operands = [
        pltpu.with_memory_space_constraint(a, pltpu.HBM)
        for a in (
            features, jnp.transpose(w_qkv, (1, 0, 2)), w_out, w_up, w_down,
            jnp.transpose(pattern, (0, 2, 1)), partner,
        )
    ]
    return pl.pallas_call(
        functools.partial(kernel, bits, slots, blk),
        out_shape=pltpu.VMEM((rows, width), BF16),
        in_specs=[any_spec] * 7 + [pl.BlockSpec(memory_space=pltpu.SMEM)],
        out_specs=pl.BlockSpec(memory_space=pltpu.VMEM),
        scratch_shapes=[
            pltpu.SMEM(partner.shape, jnp.int32),
            vm((rows, width), BF16),
            vm((3, width, width), BF16),
            vm((width, width), BF16),
            vm((width, ff), BF16),
            vm((ff, width), BF16),
            vm((slots, words, blk), jnp.int32),
            vm((width, width), BF16),
            vm((width, width), BF16),
            vm((rows, width), BF16),
            vm((slots, far * blk, width), BF16),
            vm((slots, PAIRS, 2 * HD, 2 * blk), BF16),
            vm((slots, blk, width), BF16),
            vm((slots, width, blk), BF16),
            vm((slots, blk, width), BF16),
            vm((slots, width, blk), BF16),
            vm((far, slots, blk, width), BF16),
            vm((far, slots, width, blk), BF16),
            vm((slots, width, blk), F32),
            vm((slots, H, blk), F32),
            vm((slots, H, blk), F32),
            vm((far, slots, width, blk), F32),
            vm((far, slots, H, blk), F32),
            vm((far, slots, H, blk), F32),
            vm((rows, width), BF16),
            sem((7,)),
            sem,
            sem,
            sem((slots, far)),
            sem((slots, far)),
        ],
        compiler_params=pltpu.CompilerParams(
            collective_id=0, has_side_effects=True, vmem_limit_bytes=48 * 2**20
        ),
        cost_estimate=pl.CostEstimate(
            flops=5 * 10**9, bytes_accessed=10 * 2**20, transcendentals=2 * 10**6
        ),
        name="layer",
    )(*operands, counts)


def solution(mesh):
    placed = (
        P(("nodes", "heads"), None),
        P(),
        P(),
        P(),
        P(),
        P(("nodes", "heads"), None, None),
        P(("nodes", "heads"), None),
        P(("nodes", "heads")),
    )
    return jax.shard_map(
        local, mesh=mesh, in_specs=placed, out_specs=P(("nodes", "heads"), None), check_vma=False
    )
```

```python
import functools

import jax
import jax.numpy as jnp
from jax import lax
from jax.experimental import pallas as pl
from jax.experimental.pallas import tpu as pltpu
from jax.sharding import PartitionSpec as P

D = 512
H = 8
HD = D // H
PAIRS = H // 2
LINKS = 4

epsilon = 1e-05
F32 = jnp.float32
BF16 = jnp.bfloat16


def flip(index, mask):
    return index + mask - 2 * mask * ((index // mask) % 2)


def dot_nn(a, b):
    return jnp.dot(a, b, preferred_element_type=F32)


def dot_nt(a, b):
    return lax.dot_general(a, b, (((1,), (1,)), ((), ())), preferred_element_type=F32)


def kernel(
    bits, slots, blk,
    feat_hbm, w3_hbm, wo_hbm, wu_hbm, wd_hbm, pat_hbm, partner_hbm, counts,
    out_ref,
    partner, x, w3, wo, wu, wd, pat, wqt, wvt, near, far,
    qpad, kown, vown, knear, vnear, kfar, vfar,
    ob, mb, lb, of, mf, lf, nf, nb,
    load_sem, near_send, near_recv, far_send, far_recv,
):
    node = lax.axis_index("nodes")
    core = lax.axis_index("heads")

    def target(bit):
        if bit == 0:
            return (node, flip(core, 1))
        return (flip(node, 2 ** (bit - 1)), core)

    barrier = pltpu.get_barrier_semaphore()
    for bit in bits:
        pl.semaphore_signal(
            barrier, inc=1, device_id=target(bit), device_id_type=pl.DeviceIdType.MESH
        )
    loads = []
    for i, (src, dst) in enumerate(
        [(w3_hbm, w3), (feat_hbm, x), (pat_hbm, pat), (wo_hbm, wo), (wu_hbm, wu), (wd_hbm, wd),
         (partner_hbm, partner)]
    ):
        loads.append(pltpu.make_async_copy(src, dst, load_sem.at[i]))
        loads[-1].start()

    pl.semaphore_wait(barrier, LINKS)

    far_copies = []
    near_copy = pltpu.make_async_remote_copy(
        src_ref=feat_hbm, dst_ref=near, send_sem=near_send, recv_sem=near_recv,
        device_id=target(bits[0]), device_id_type=pl.DeviceIdType.MESH,
    )
    pieces = [(0, slots - 1), (slots - 1, 1)]
    for n, (first, count) in enumerate(pieces):
        row = []
        for l in range(LINKS - 1):
            row.append(pltpu.make_async_remote_copy(
                src_ref=feat_hbm.at[pl.ds(first * blk, count * blk)],
                dst_ref=far.at[pl.ds(((LINKS - 1) * first + l * count) * blk, count * blk)],
                send_sem=far_send.at[n, l], recv_sem=far_recv.at[n, l],
                device_id=target(bits[l + 1]), device_id_type=pl.DeviceIdType.MESH,
            ))
            row[-1].start()
        far_copies.append(row)
        if n == 0:
            near_copy.start()

    loads[0].wait()
    loads[1].wait()
    wqt[...] = w3[0].T
    wvt[...] = w3[2].T
    own = x[...]
    qt = dot_nt(wqt[...], own).astype(BF16) * jnp.asarray(1.0 / HD**0.5, BF16)
    zero = jnp.zeros((HD, blk), BF16)
    for s in range(slots):
        for p in range(PAIRS):
            a = qt[2 * p * HD : (2 * p + 1) * HD, s * blk : (s + 1) * blk]
            b = qt[(2 * p + 1) * HD : (2 * p + 2) * HD, s * blk : (s + 1) * blk]
            qpad[s, p] = jnp.concatenate(
                [jnp.concatenate([a, zero], 1), jnp.concatenate([zero, b], 1)], 0
            )

    def project(rows, put_k, put_v):
        k = dot_nn(rows, w3[1]).astype(BF16)
        v = dot_nt(wvt[...], rows).astype(BF16)
        for i in range(slots):
            put_k(i, k[i * blk : (i + 1) * blk])
            put_v(i, v[:, i * blk : (i + 1) * blk])

    def setter(ref, where):
        def put(i, value):
            ref[where(i)] = value
        return put

    project(own, setter(kown, lambda i: i), setter(vown, lambda i: i))
    near_copy.wait_recv()
    project(near[...], setter(knear, lambda i: i), setter(vnear, lambda i: i))
    for i in (2, 6):
        loads[i].wait()

    def run(units):
        waiting = None
        scores = units[0][0]()
        for i, (_, values, put) in enumerate(units):
            following = units[i + 1][0]() if i + 1 < len(units) else None
            m = functools.reduce(jnp.maximum, [jnp.max(a, 0, keepdims=True) for a in scores])
            expo = [jnp.exp(a - m) for a in scores]
            l = functools.reduce(jnp.add, [jnp.sum(a, 0, keepdims=True) for a in expo])
            expo = [a.astype(BF16) for a in expo]
            if waiting is not None:
                waiting()
            waiting = functools.partial(
                lambda values, put, expo, m, l: put(values(expo), m, l), values, put, expo, m, l
            )
            scores = following
        waiting()

    def keep(o_ref, m_ref, l_ref, at, p, o, m, l):
        o_ref[at + (pl.ds(2 * p * HD, HD),)] = o[:HD, :blk]
        o_ref[at + (pl.ds((2 * p + 1) * HD, HD),)] = o[HD:, blk:]
        for half in range(2):
            cols = slice(half * blk, (half + 1) * blk)
            m_ref[at + (pl.ds(2 * p + half, 1),)] = m[:, cols]
            l_ref[at + (pl.ds(2 * p + half, 1),)] = l[:, cols]

    bit_row = lax.broadcasted_iota(jnp.int32, (16, blk), 0)
    key_at = lax.broadcasted_iota(jnp.int32, (blk, blk), 0)
    query_at = lax.broadcasted_iota(jnp.int32, (blk, blk), 1)
    units = []
    for s in range(slots):
        words = pat[s]
        picked = jnp.concatenate(
            [
                jnp.right_shift(jnp.broadcast_to(words[w : w + 1], (16, blk)), bit_row) & 1
                for w in range(blk // 16)
            ],
            0,
        )
        bias = jnp.where((picked == 1) | (key_at == query_at), 0.0, -1e30).astype(F32)
        bias = jnp.concatenate([bias, bias], 1)
        linked = partner[s, 0]
        k1 = knear[linked]
        v1 = vnear[linked]
        for p in range(PAIRS):
            cols = slice(2 * p * HD, 2 * (p + 1) * HD)

            def scores(s=s, p=p, cols=cols, bias=bias, k1=k1):
                q = qpad[s, p]
                return [dot_nn(kown[s, :, cols], q) + bias, dot_nn(k1[:, cols], q)]

            def values(e, s=s, cols=cols, v1=v1):
                return dot_nn(
                    jnp.concatenate([vown[s, cols], v1[cols]], 1), jnp.concatenate(e, 0)
                )

            units.append((scores, values, functools.partial(keep, ob, mb, lb, (s,), p)))
    run(units)

    for i in (3, 4, 5):
        loads[i].wait()

    ranks, order = [], []
    for l in range(1, LINKS):
        named = [partner[s, l] for s in range(slots)]
        rank = []
        for s in range(slots):
            r = jnp.int32(0)
            for t in range(slots):
                if t != s:
                    before = named[t] <= named[s] if t < s else named[t] < named[s]
                    r = r + jnp.where(before, 1, 0).astype(jnp.int32)
            rank.append(r)
        at = []
        for j in range(slots):
            slot, block = jnp.int32(0), jnp.int32(0)
            for s in range(slots):
                slot = jnp.where(rank[s] == j, s, slot)
                block = jnp.where(rank[s] == j, named[s], block)
            at.append((slot, block))
        ranks.append(rank)
        order.append(at)

    for n, (first, count) in enumerate(pieces):
        for l in range(LINKS - 1):
            far_copies[n][l].wait_recv()
        rows = far[pl.ds((LINKS - 1) * first * blk, (LINKS - 1) * count * blk)]
        k = dot_nn(rows, w3[1]).astype(BF16)
        v = dot_nt(wvt[...], rows).astype(BF16)
        for l in range(LINKS - 1):
            for i in range(count):
                at = (l * count + i) * blk
                kfar[l, first + i] = k[at : at + blk]
                vfar[l, first + i] = v[:, at : at + blk]
        units = []
        for j in range(first, first + count):
            for l in range(LINKS - 1):
                slot, block = order[l][j]
                for p in range(PAIRS):
                    cols = slice(2 * p * HD, 2 * (p + 1) * HD)

                    def scores(l=l, slot=slot, block=block, p=p, cols=cols):
                        return [dot_nn(kfar[l, block, :, cols], qpad[slot, p])]

                    def values(e, l=l, block=block, cols=cols):
                        return dot_nn(vfar[l, block, cols], e[0])

                    units.append((scores, values, functools.partial(keep, of, mf, lf, (l, j), p)))
        run(units)

    for s in range(slots):
        ms = [mb[s]] + [mf[l, ranks[l][s]] for l in range(LINKS - 1)]
        ls = [lb[s]] + [lf[l, ranks[l][s]] for l in range(LINKS - 1)]
        os = [ob[s]] + [of[l, ranks[l][s]] for l in range(LINKS - 1)]
        top = functools.reduce(jnp.maximum, ms)
        scale = [jnp.exp(m - top) for m in ms]
        total = functools.reduce(jnp.add, [a * b for a, b in zip(scale, ls)])
        scale = [a / total for a in scale]
        heads = []
        for h in range(H):
            heads.append(functools.reduce(
                jnp.add,
                [o[h * HD : (h + 1) * HD] * a[h : h + 1] for o, a in zip(os, scale)],
            ))
        joined = jnp.concatenate(heads, 0)
        here = pl.ds(s * blk, blk)
        resid = x[here].astype(F32) + dot_nn(joined.astype(BF16).T, wo[...])
        mean = jnp.mean(resid, 1, keepdims=True)
        var = jnp.mean(resid * resid, 1, keepdims=True) - mean * mean
        normed = (resid - mean) * lax.rsqrt(var + epsilon)
        nf[here] = normed
        nb[here] = normed.astype(BF16)

    hidden = jnp.maximum(dot_nn(nb[...], wu[...]), 0.0).astype(BF16)
    mixed = nf[...] + dot_nn(hidden, wd[...])
    live = counts[0]
    for s in range(slots):
        part = mixed[s * blk : (s + 1) * blk]
        out_ref[pl.ds(s * blk, blk)] = jnp.where(s < live, part, 0.0).astype(BF16)

    near_copy.wait_send()
    for row in far_copies:
        for copy in row:
            copy.wait_send()


def local(features, w_qkv, w_out, w_up, w_down, pattern, partner, counts):
    rows, width = features.shape
    slots = partner.shape[0]
    blk = rows // slots
    ff = w_up.shape[1]
    words = pattern.shape[2]
    log_size = (lax.axis_size("nodes") * lax.axis_size("heads")).bit_length() - 1
    bits = [i * log_size // 4 for i in range(LINKS)]
    far = LINKS - 1
    any_spec = pl.BlockSpec(memory_space=pl.ANY)
    vm = pltpu.VMEM
    sem = pltpu.SemaphoreType.DMA
    operands = [
        pltpu.with_memory_space_constraint(a, pltpu.HBM)
        for a in (
            features, jnp.transpose(w_qkv, (1, 0, 2)), w_out, w_up, w_down,
            jnp.transpose(pattern, (0, 2, 1)), partner,
        )
    ]
    return pl.pallas_call(
        functools.partial(kernel, bits, slots, blk),
        out_shape=pltpu.VMEM((rows, width), BF16),
        in_specs=[any_spec] * 7 + [pl.BlockSpec(memory_space=pltpu.SMEM)],
        out_specs=pl.BlockSpec(memory_space=pltpu.VMEM),
        scratch_shapes=[
            pltpu.SMEM(partner.shape, jnp.int32),
            vm((rows, width), BF16),
            vm((3, width, width), BF16),
            vm((width, width), BF16),
            vm((width, ff), BF16),
            vm((ff, width), BF16),
            vm((slots, words, blk), jnp.int32),
            vm((width, width), BF16),
            vm((width, width), BF16),
            vm((rows, width), BF16),
            vm((slots * far * blk, width), BF16),
            vm((slots, PAIRS, 2 * HD, 2 * blk), BF16),
            vm((slots, blk, width), BF16),
            vm((slots, width, blk), BF16),
            vm((slots, blk, width), BF16),
            vm((slots, width, blk), BF16),
            vm((far, slots, blk, width), BF16),
            vm((far, slots, width, blk), BF16),
            vm((slots, width, blk), F32),
            vm((slots, H, blk), F32),
            vm((slots, H, blk), F32),
            vm((far, slots, width, blk), F32),
            vm((far, slots, H, blk), F32),
            vm((far, slots, H, blk), F32),
            vm((rows, width), F32),
            vm((rows, width), BF16),
            sem((7,)),
            sem,
            sem,
            sem((2, far)),
            sem((2, far)),
        ],
        compiler_params=pltpu.CompilerParams(
            collective_id=0, has_side_effects=True, vmem_limit_bytes=48 * 2**20
        ),
        cost_estimate=pl.CostEstimate(
            flops=5 * 10**9, bytes_accessed=10 * 2**20, transcendentals=2 * 10**6
        ),
        name="layer",
    )(*operands, counts)


def solution(mesh):
    placed = (
        P(("nodes", "heads"), None),
        P(),
        P(),
        P(),
        P(),
        P(("nodes", "heads"), None, None),
        P(("nodes", "heads"), None),
        P(("nodes", "heads")),
    )
    return jax.shard_map(
        local, mesh=mesh, in_specs=placed, out_specs=P(("nodes", "heads"), None), check_vma=False
    )
```

```python
import functools

import jax
import jax.numpy as jnp
from jax import lax
from jax.experimental import pallas as pl
from jax.experimental.pallas import tpu as pltpu
from jax.sharding import PartitionSpec as P

D = 512
H = 8
HD = D // H
PAIRS = H // 2
LINKS = 4

epsilon = 1e-05
F32 = jnp.float32
BF16 = jnp.bfloat16


def flip(index, mask):
    return index + mask - 2 * mask * ((index // mask) % 2)


def dot_nn(a, b):
    return jnp.dot(a, b, preferred_element_type=F32)


def dot_nt(a, b):
    return lax.dot_general(a, b, (((1,), (1,)), ((), ())), preferred_element_type=F32)


def kernel(
    bits, slots, blk,
    feat_hbm, w3_hbm, wo_hbm, wu_hbm, wd_hbm, pat_hbm, partner_hbm, counts,
    out_ref,
    partner, x, w3, wo, wu, wd, pat, wqt, wvt, near, far,
    qpad, kown, vown, knear, vnear, kfar, vfar,
    ob, mb, lb, of, mf, lf, nf, nb,
    load_sem, near_send, near_recv, far_send, far_recv,
):
    node = lax.axis_index("nodes")
    core = lax.axis_index("heads")

    def target(bit):
        if bit == 0:
            return (node, flip(core, 1))
        return (flip(node, 2 ** (bit - 1)), core)

    loads = []
    for i, (src, dst) in enumerate(
        [(w3_hbm, w3), (feat_hbm, x), (pat_hbm, pat), (wo_hbm, wo), (wu_hbm, wu), (wd_hbm, wd),
         (partner_hbm, partner)]
    ):
        loads.append(pltpu.make_async_copy(src, dst, load_sem.at[i]))
        loads[-1].start()

    barrier = pltpu.get_barrier_semaphore()
    for bit in bits:
        pl.semaphore_signal(
            barrier, inc=1, device_id=target(bit), device_id_type=pl.DeviceIdType.MESH
        )
    pl.semaphore_wait(barrier, LINKS)

    far_copies = []
    near_copy = pltpu.make_async_remote_copy(
        src_ref=feat_hbm, dst_ref=near, send_sem=near_send, recv_sem=near_recv,
        device_id=target(bits[0]), device_id_type=pl.DeviceIdType.MESH,
    )
    for j in range(slots):
        row = []
        for l in range(LINKS - 1):
            row.append(pltpu.make_async_remote_copy(
                src_ref=feat_hbm.at[pl.ds(j * blk, blk)],
                dst_ref=far.at[j, pl.ds(l * blk, blk)],
                send_sem=far_send.at[j, l], recv_sem=far_recv.at[j, l],
                device_id=target(bits[l + 1]), device_id_type=pl.DeviceIdType.MESH,
            ))
            if j < 2:
                row[-1].start()
        far_copies.append(row)
        if j == 0:
            near_copy.start()

    loads[0].wait()
    loads[1].wait()
    wqt[...] = w3[0].T
    wvt[...] = w3[2].T
    own = x[...]
    qt = dot_nt(wqt[...], own).astype(BF16) * jnp.asarray(1.0 / HD**0.5, BF16)
    zero = jnp.zeros((HD, blk), BF16)
    for s in range(slots):
        for p in range(PAIRS):
            a = qt[2 * p * HD : (2 * p + 1) * HD, s * blk : (s + 1) * blk]
            b = qt[(2 * p + 1) * HD : (2 * p + 2) * HD, s * blk : (s + 1) * blk]
            qpad[s, p] = jnp.concatenate(
                [jnp.concatenate([a, zero], 1), jnp.concatenate([zero, b], 1)], 0
            )

    def project(rows, put_k, put_v):
        k = dot_nn(rows, w3[1]).astype(BF16)
        v = dot_nt(wvt[...], rows).astype(BF16)
        for i in range(slots):
            put_k(i, k[i * blk : (i + 1) * blk])
            put_v(i, v[:, i * blk : (i + 1) * blk])

    def setter(ref, where):
        def put(i, value):
            ref[where(i)] = value
        return put

    project(own, setter(kown, lambda i: i), setter(vown, lambda i: i))
    near_copy.wait_recv()
    project(near[...], setter(knear, lambda i: i), setter(vnear, lambda i: i))
    for i in (2, 6):
        loads[i].wait()

    def run(units):
        ahead, behind = 2, 2
        waiting = []
        ready = [unit[0]() for unit in units[:ahead]]
        for i, (_, values, put) in enumerate(units):
            if i + ahead < len(units):
                ready.append(units[i + ahead][0]())
            scores = ready.pop(0)
            m = functools.reduce(jnp.maximum, [jnp.max(a, 0, keepdims=True) for a in scores])
            expo = [jnp.exp(a - m) for a in scores]
            l = functools.reduce(jnp.add, [jnp.sum(a, 0, keepdims=True) for a in expo])
            expo = [a.astype(BF16) for a in expo]
            if len(waiting) == behind:
                put_first, values_first, *first = waiting.pop(0)
                put_first(values_first(first[0]), first[1], first[2])
            waiting.append((put, values, expo, m, l))
        for put, values, expo, m, l in waiting:
            put(values(expo), m, l)

    def keep(o_ref, m_ref, l_ref, at, p, o, m, l):
        o_ref[at + (pl.ds(2 * p * HD, HD),)] = o[:HD, :blk]
        o_ref[at + (pl.ds((2 * p + 1) * HD, HD),)] = o[HD:, blk:]
        for half in range(2):
            cols = slice(half * blk, (half + 1) * blk)
            m_ref[at + (pl.ds(2 * p + half, 1),)] = m[:, cols]
            l_ref[at + (pl.ds(2 * p + half, 1),)] = l[:, cols]

    bit_row = lax.broadcasted_iota(jnp.int32, (16, blk), 0)
    key_at = lax.broadcasted_iota(jnp.int32, (blk, blk), 0)
    query_at = lax.broadcasted_iota(jnp.int32, (blk, blk), 1)
    units = []
    for s in range(slots):
        words = pat[s]
        picked = jnp.concatenate(
            [
                jnp.right_shift(jnp.broadcast_to(words[w : w + 1], (16, blk)), bit_row) & 1
                for w in range(blk // 16)
            ],
            0,
        )
        bias = jnp.where((picked == 1) | (key_at == query_at), 0.0, -1e30).astype(F32)
        bias = jnp.concatenate([bias, bias], 1)
        linked = partner[s, 0]
        k1 = knear[linked]
        v1 = vnear[linked]
        for p in range(PAIRS):
            cols = slice(2 * p * HD, 2 * (p + 1) * HD)

            def scores(s=s, p=p, cols=cols, bias=bias, k1=k1):
                q = qpad[s, p]
                return [dot_nn(kown[s, :, cols], q) + bias, dot_nn(k1[:, cols], q)]

            def values(e, s=s, cols=cols, v1=v1):
                return dot_nn(
                    jnp.concatenate([vown[s, cols], v1[cols]], 1), jnp.concatenate(e, 0)
                )

            units.append((scores, values, functools.partial(keep, ob, mb, lb, (s,), p)))
    run(units)

    for i in (3, 4, 5):
        loads[i].wait()

    for j in range(2, slots):
        for l in range(LINKS - 1):
            far_copies[j - 2][l].wait_send()
            far_copies[j][l].start()

    ranks, order = [], []
    for l in range(1, LINKS):
        named = [partner[s, l] for s in range(slots)]
        rank = []
        for s in range(slots):
            r = jnp.int32(0)
            for t in range(slots):
                if t != s:
                    before = named[t] <= named[s] if t < s else named[t] < named[s]
                    r = r + jnp.where(before, 1, 0).astype(jnp.int32)
            rank.append(r)
        at = []
        for j in range(slots):
            slot, block = jnp.int32(0), jnp.int32(0)
            for s in range(slots):
                slot = jnp.where(rank[s] == j, s, slot)
                block = jnp.where(rank[s] == j, named[s], block)
            at.append((slot, block))
        ranks.append(rank)
        order.append(at)

    for j in range(slots):
        for l in range(LINKS - 1):
            far_copies[j][l].wait_recv()
        rows = far[j]
        k = dot_nn(rows, w3[1]).astype(BF16)
        v = dot_nt(wvt[...], rows).astype(BF16)
        for l in range(LINKS - 1):
            kfar[l, j] = k[l * blk : (l + 1) * blk]
            vfar[l, j] = v[:, l * blk : (l + 1) * blk]
        units = []
        for l in range(LINKS - 1):
            slot, block = order[l][j]
            for p in range(PAIRS):
                cols = slice(2 * p * HD, 2 * (p + 1) * HD)

                def scores(l=l, slot=slot, block=block, p=p, cols=cols):
                    return [dot_nn(kfar[l, block, :, cols], qpad[slot, p])]

                def values(e, l=l, block=block, cols=cols):
                    return dot_nn(vfar[l, block, cols], e[0])

                units.append((scores, values, functools.partial(keep, of, mf, lf, (l, j), p)))
        run(units)

    for s in range(slots):
        ms = [mb[s]] + [mf[l, ranks[l][s]] for l in range(LINKS - 1)]
        ls = [lb[s]] + [lf[l, ranks[l][s]] for l in range(LINKS - 1)]
        os = [ob[s]] + [of[l, ranks[l][s]] for l in range(LINKS - 1)]
        top = functools.reduce(jnp.maximum, ms)
        scale = [jnp.exp(m - top) for m in ms]
        total = functools.reduce(jnp.add, [a * b for a, b in zip(scale, ls)])
        scale = [a / total for a in scale]
        heads = []
        for h in range(H):
            heads.append(functools.reduce(
                jnp.add,
                [o[h * HD : (h + 1) * HD] * a[h : h + 1] for o, a in zip(os, scale)],
            ))
        joined = jnp.concatenate(heads, 0)
        here = pl.ds(s * blk, blk)
        resid = x[here].astype(F32) + dot_nn(joined.astype(BF16).T, wo[...])
        mean = jnp.mean(resid, 1, keepdims=True)
        var = jnp.mean(resid * resid, 1, keepdims=True) - mean * mean
        normed = (resid - mean) * lax.rsqrt(var + epsilon)
        nf[here] = normed
        nb[here] = normed.astype(BF16)

    hidden = jnp.maximum(dot_nn(nb[...], wu[...]), 0.0).astype(BF16)
    mixed = nf[...] + dot_nn(hidden, wd[...])
    live = counts[0]
    for s in range(slots):
        part = mixed[s * blk : (s + 1) * blk]
        out_ref[pl.ds(s * blk, blk)] = jnp.where(s < live, part, 0.0).astype(BF16)

    near_copy.wait_send()
    for row in far_copies[max(slots - 2, 0):]:
        for copy in row:
            copy.wait_send()


def local(features, w_qkv, w_out, w_up, w_down, pattern, partner, counts):
    rows, width = features.shape
    slots = partner.shape[0]
    blk = rows // slots
    ff = w_up.shape[1]
    words = pattern.shape[2]
    log_size = (lax.axis_size("nodes") * lax.axis_size("heads")).bit_length() - 1
    bits = [i * log_size // 4 for i in range(LINKS)]
    far = LINKS - 1
    any_spec = pl.BlockSpec(memory_space=pl.ANY)
    vm = pltpu.VMEM
    sem = pltpu.SemaphoreType.DMA
    operands = [
        pltpu.with_memory_space_constraint(a, pltpu.HBM)
        for a in (
            features, jnp.transpose(w_qkv, (1, 0, 2)), w_out, w_up, w_down,
            jnp.transpose(pattern, (0, 2, 1)), partner,
        )
    ]
    return pl.pallas_call(
        functools.partial(kernel, bits, slots, blk),
        out_shape=pltpu.VMEM((rows, width), BF16),
        in_specs=[any_spec] * 7 + [pl.BlockSpec(memory_space=pltpu.SMEM)],
        out_specs=pl.BlockSpec(memory_space=pltpu.VMEM),
        scratch_shapes=[
            pltpu.SMEM(partner.shape, jnp.int32),
            vm((rows, width), BF16),
            vm((3, width, width), BF16),
            vm((width, width), BF16),
            vm((width, ff), BF16),
            vm((ff, width), BF16),
            vm((slots, words, blk), jnp.int32),
            vm((width, width), BF16),
            vm((width, width), BF16),
            vm((rows, width), BF16),
            vm((slots, far * blk, width), BF16),
            vm((slots, PAIRS, 2 * HD, 2 * blk), BF16),
            vm((slots, blk, width), BF16),
            vm((slots, width, blk), BF16),
            vm((slots, blk, width), BF16),
            vm((slots, width, blk), BF16),
            vm((far, slots, blk, width), BF16),
            vm((far, slots, width, blk), BF16),
            vm((slots, width, blk), F32),
            vm((slots, H, blk), F32),
            vm((slots, H, blk), F32),
            vm((far, slots, width, blk), F32),
            vm((far, slots, H, blk), F32),
            vm((far, slots, H, blk), F32),
            vm((rows, width), F32),
            vm((rows, width), BF16),
            sem((7,)),
            sem,
            sem,
            sem((slots, far)),
            sem((slots, far)),
        ],
        compiler_params=pltpu.CompilerParams(
            collective_id=0, has_side_effects=True, vmem_limit_bytes=48 * 2**20
        ),
        cost_estimate=pl.CostEstimate(
            flops=5 * 10**9, bytes_accessed=10 * 2**20, transcendentals=2 * 10**6
        ),
        name="layer",
    )(*operands, counts)


def solution(mesh):
    placed = (
        P(("nodes", "heads"), None),
        P(),
        P(),
        P(),
        P(),
        P(("nodes", "heads"), None, None),
        P(("nodes", "heads"), None),
        P(("nodes", "heads")),
    )
    return jax.shard_map(
        local, mesh=mesh, in_specs=placed, out_specs=P(("nodes", "heads"), None), check_vma=False
    )
```
